256 devices in a mesh: gx: 32 (over x, z), gy: 8 (over y, core).
Axes of the slice: x: 4, y: 4, z: 8, core: 2. Of those that a mesh axis runs over, the one named last changes fastest.
Arguments:
- order_params: float32 [24, 12, 256, 1024], P(None, None, 'gx', 'gy'), may hold values from 0 to 1, as said below
- grain_ids: int32 [32, 8, 24], P('gx', 'gy'), may hold values from -1 to 9215, as said below
- channel_maps: int32 [32, 8, 4, 24], P('gx', 'gy'), may hold values from -1 to 23, as said below
- zplanes: int32 [2, 256, 1024], P(None, 'gx', 'gy'), may hold values from 0 to 9215, as said below
Outputs:
- evolved: float32 [24, 12, 256, 1024], P(None, None, 'gx', 'gy')
The draws below stay inside these ranges and needn't reach their ends.
Inputs may be any that keep to these rules, and one draw needn't show every extreme that they name: `order_params`: zero in every slot whose grain id is -1. `grain_ids`: grain ids are distinct within a block; -1 marks an empty slot. `channel_maps`: A non-negative entry for face f of a block names the adjacent block's slot with the same grain; the entries for face f of a block and for the opposite face of the adjacent block are inverse one-to-one matchings. At most 6 slots of a block have an entry for any one face, and in every draw some face of some block has exactly 6. A slot has an entry for at most one face. `zplanes`: each cell names one of the non-negative grain ids of its block.
All inputs are finite; a program needn't handle non-finite values.
Results may differ from the reference program's by a relative error of at most 0.00018.
Values sent between devices are 32-bit elements; how exact they have to be, the bound alone decides.
A program may use at most 64 MiB of HBM per device.

```python
import jax
import jax.numpy as jnp
from jax import lax

SLOTS = 24
SHARED = 6
CZ = 12
CX = 8
CY = 128
STEPS = 3
PX = 32
PY = 8
NX = 256
NY = 1024


def grain_layout(key):
    pair_x = jax.random.randint(jax.random.fold_in(key, 11), (PX, PY), 1, SHARED + 1)
    pair_x = pair_x.at[0, 0].set(SHARED)
    pair_x = pair_x.at[PX - 1, 0].set(1)
    pair_y = jax.random.randint(jax.random.fold_in(key, 12), (PX, PY), 1, SHARED + 1)
    pair_y = pair_y.at[0, 0].set(SHARED)
    pair_y = pair_y.at[PX - 1, PY - 1].set(1)
    counts = jnp.stack([jnp.roll(pair_x, 1, 0), pair_x, jnp.roll(pair_y, 1, 1), pair_y], axis=2)
    within = jnp.arange(SHARED, dtype=jnp.int32)
    linked = within[None, None, None, :] < counts[..., None]
    rows_grid = jnp.arange(PX, dtype=jnp.int32)[:, None] + jnp.zeros((PX, PY), jnp.int32)
    cols_grid = jnp.arange(PY, dtype=jnp.int32)[None, :] + jnp.zeros((PX, PY), jnp.int32)
    face_x_up = rows_grid * PY + cols_grid
    face_x_low = (rows_grid - 1) % PX * PY + cols_grid
    face_y_up = PX * PY + rows_grid * PY + cols_grid
    face_y_low = PX * PY + rows_grid * PY + (cols_grid - 1) % PY
    face_code = jnp.stack([face_x_low, face_x_up, face_y_low, face_y_up], axis=2)
    shared_code = face_code[..., None] * SHARED + within
    block_code = (rows_grid * PY + cols_grid)[..., None] * 4 + jnp.arange(4, dtype=jnp.int32)
    own_code = 2 * PX * PY * SHARED + block_code[..., None] * SHARED + within
    extra = jax.random.randint(jax.random.fold_in(key, 13), (PX, PY, 4, SHARED), 0, 2)
    extra = extra.at[PX - 1, PY - 1, 3, SHARED - 1].set(1)
    extra = extra.at[0, 0, 0, SHARED - 1].set(0)
    codes = jnp.where(linked, shared_code, jnp.where(extra == 1, own_code, -1)).reshape(PX, PY, SLOTS)
    keys = jax.random.split(jax.random.fold_in(key, 14), PX * PY)
    order = jax.vmap(lambda one_key: jax.random.permutation(one_key, SLOTS))(keys)
    order = order.reshape(PX, PY, SLOTS).astype(jnp.int32)
    inverse = jnp.argsort(order, axis=2, stable=True).astype(jnp.int32)
    slot_grains = jnp.take_along_axis(codes, inverse, axis=2)
    segments = order.reshape(PX, PY, 4, SHARED)
    partner = jnp.stack([jnp.roll(segments[:, :, 1], 1, 0), jnp.roll(segments[:, :, 0], -1, 0), jnp.roll(segments[:, :, 3], 1, 1), jnp.roll(segments[:, :, 2], -1, 1)], axis=2)
    target = jnp.where(linked, partner, -1)
    same_face = jnp.arange(4)[:, None] == jnp.arange(4)[None, :]
    table = jnp.where(same_face[None, None, :, :, None], target[:, :, None, :, :], -1)
    table = table.reshape(PX, PY, 4, SLOTS).astype(jnp.int32)
    face_maps = jnp.take_along_axis(table, inverse[:, :, None, :], axis=3)
    return (slot_grains.astype(jnp.int32), face_maps.astype(jnp.int32))


def draw_grain_ids(key, part):
    slot_grains, face_maps = grain_layout(key)
    return slot_grains


def draw_channel_maps(key, part):
    slot_grains, face_maps = grain_layout(key)
    return face_maps


def draw_zplanes(key, part):
    slot_grains, face_maps = grain_layout(key)
    active = (slot_grains >= 0).astype(jnp.int32)
    ranks = jnp.cumsum(active, axis=2) - active
    live = jnp.sum(active, axis=2)
    cell_live = jnp.repeat(jnp.repeat(live, CX, axis=0), CY, axis=1)
    picks = jax.random.randint(jax.random.fold_in(key, 15), (2, NX, NY), 0, cell_live[None])
    cell_grains = jnp.repeat(jnp.repeat(slot_grains, CX, axis=0), CY, axis=1)
    cell_ranks = jnp.repeat(jnp.repeat(ranks, CX, axis=0), CY, axis=1)
    cell_active = jnp.repeat(jnp.repeat(active, CX, axis=0), CY, axis=1)
    chosen = (cell_ranks[None] == picks[..., None]) & (cell_active[None] == 1)
    planes = jnp.sum(jnp.where(chosen, cell_grains[None], 0), axis=3)
    top_grain = jnp.max(slot_grains[PX - 1, PY - 1])
    big_code = 6 * PX * PY * SHARED
    low_grain = jnp.min(jnp.where(slot_grains[0, 0] >= 0, slot_grains[0, 0], big_code))
    planes = planes.at[0, NX - 1, NY - 1].set(top_grain)
    planes = planes.at[1, 0, 0].set(low_grain)
    return planes.astype(jnp.int32)


def draw_order_params(key, part):
    slot_grains, face_maps = grain_layout(key)
    active = (slot_grains >= 0).astype(jnp.float32)
    cell_active = jnp.repeat(jnp.repeat(active, CX, axis=0), CY, axis=1)
    cell_active = jnp.transpose(cell_active, (2, 0, 1))[:, None, :, :]
    raw = jax.random.uniform(jax.random.fold_in(key, 16), (SLOTS, CZ, NX, NY), jnp.float32)
    values = raw ** 3
    return (values * cell_active).astype(jnp.float32)


def setup_inputs(seed: int = 0) -> dict:
    key_list = jax.random.split(jax.random.key(seed), 5)
    return {
        "order_params": draw_order_params(jax.random.fold_in(key_list[4], 71), 0),
        "grain_ids": draw_grain_ids(jax.random.fold_in(key_list[4], 71), 0),
        "channel_maps": draw_channel_maps(jax.random.fold_in(key_list[4], 71), 0),
        "zplanes": draw_zplanes(jax.random.fold_in(key_list[4], 71), 0),
    }


time_step = 0.05
mobility = 1.0
alpha_coef = 1.0
beta_coef = 1.0
gamma_coef = 1.5
kappa_coef = 2.0


def remap(plane, index):
    valid = index >= 0
    safe = jnp.where(valid, index, 0).astype(jnp.int32)
    gather_index = jnp.broadcast_to(jnp.transpose(safe, (2, 0, 1))[:, None, :, :, None], plane.shape)
    picked = jnp.take_along_axis(plane, gather_index, axis=0)
    keep = jnp.transpose(valid, (2, 0, 1))[:, None, :, :, None]
    return jnp.where(keep, picked, jnp.float32(0.0))


def advance(field6, channel_maps, frozen6):
    lower_x = remap(jnp.roll(field6[:, :, :, -1], 1, axis=2), channel_maps[:, :, 0])
    upper_x = remap(jnp.roll(field6[:, :, :, 0], -1, axis=2), channel_maps[:, :, 1])
    last_y = jnp.transpose(field6[..., -1], (0, 1, 2, 4, 3))
    first_y = jnp.transpose(field6[..., 0], (0, 1, 2, 4, 3))
    lower_y = remap(jnp.roll(last_y, 1, axis=3), channel_maps[:, :, 2])
    upper_y = remap(jnp.roll(first_y, -1, axis=3), channel_maps[:, :, 3])
    total = jnp.sum(field6 * field6, axis=0)

    def one_slot(pieces):
        value, low_x, up_x, low_y, up_y, planes = pieces
        low_y = jnp.transpose(low_y, (0, 1, 3, 2))
        up_y = jnp.transpose(up_y, (0, 1, 3, 2))
        above_x = jnp.concatenate([value[:, :, 1:], up_x[:, :, None]], axis=2)
        below_x = jnp.concatenate([low_x[:, :, None], value[:, :, :-1]], axis=2)
        above_y = jnp.concatenate([value[..., 1:], up_y[..., None]], axis=4)
        below_y = jnp.concatenate([low_y[..., None], value[..., :-1]], axis=4)
        above_z = jnp.concatenate([value[1:], planes[1][None]], axis=0)
        below_z = jnp.concatenate([planes[0][None], value[:-1]], axis=0)
        laplace = above_x + below_x + above_y + below_y + above_z + below_z - 6.0 * value
        rate = (-alpha_coef * value + beta_coef * value ** 3
                + 2.0 * gamma_coef * value * (total - value * value) - kappa_coef * laplace)
        return value - time_step * mobility * rate

    return lax.map(one_slot, (field6, lower_x, upper_x, lower_y, upper_y, frozen6))


def reference(order_params, grain_ids, channel_maps, zplanes):
    field6 = order_params.reshape(SLOTS, CZ, PX, CX, PY, CY)
    planes6 = zplanes.reshape(2, PX, CX, PY, CY)
    slot_codes = jnp.transpose(grain_ids, (2, 0, 1))[:, None, :, None, :, None]
    frozen6 = ((planes6[None] == slot_codes) & (slot_codes >= 0)).astype(jnp.float32)
    for repeat_index in range(STEPS):
        field6 = advance(field6, channel_maps, frozen6)
    return field6.reshape(SLOTS, CZ, NX, NY)
```

```python
import functools

import jax
import jax.numpy as jnp
from jax import lax
from jax.experimental import pallas as pl
from jax.experimental.pallas import tpu as pltpu
from jax.sharding import PartitionSpec as P

STEPS = 3
SHARED = 6
FACES = 4
MESH = pl.DeviceIdType.MESH

SELF = 0.45
TOTAL = 0.15
LINK = 0.1


def kernel(slots, depth, nx, ny, tab, planes, start, out, field, local, halo, send_x, recv_x, send_y, recv_y,
           in_sem, send_sem, recv_sem):
    rows, cols = 8, 128
    i, j = lax.axis_index("gx"), lax.axis_index("gy")
    across = (
        (lax.rem(i + nx - 1, nx), j),
        (lax.rem(i + 1, nx), j),
        (i, lax.rem(j + ny - 1, ny)),
        (i, lax.rem(j + 1, ny)),
    )
    barrier = pltpu.get_barrier_semaphore()
    for device in across:
        pl.semaphore_signal(barrier, inc=1, device_id=device, device_id_type=MESH)
    load = pltpu.make_async_copy(start, field, in_sem)
    load.start()

    row = lax.broadcasted_iota(jnp.int32, (rows, cols), 0)
    col = lax.broadcasted_iota(jnp.int32, (rows, cols), 1)
    zero = jnp.zeros((rows, cols), jnp.float32)

    def tile(slot, layer):
        return slot * depth + layer

    def clear(slot, carry):
        for layer in range(depth):
            halo[tile(slot, layer)] = zero
        return carry

    lax.fori_loop(0, slots + 1, clear, 0)

    def copy(step, face):
        source, target = (send_x, recv_x) if face < 2 else (send_y, recv_y)
        lane = face % 2
        return pltpu.make_async_remote_copy(
            src_ref=source.at[step, lane],
            dst_ref=target.at[step, 1 - lane],
            send_sem=send_sem.at[step, face],
            recv_sem=recv_sem.at[step, face ^ 1],
            device_id=across[face],
            device_id_type=MESH,
        )

    def arrival(step, face):
        target = recv_x if face < 2 else recv_y
        return pltpu.make_async_remote_copy(
            src_ref=target.at[step, face % 2],
            dst_ref=target.at[step, face % 2],
            send_sem=send_sem.at[step, face],
            recv_sem=recv_sem.at[step, face],
            device_id=across[face],
            device_id_type=MESH,
        )

    def pack_x(step, source):
        for face in range(2):
            edge = 0 if face == 0 else rows - 1
            for k in range(SHARED):
                slot = tab[32 + face * SHARED + k]
                for layer in range(depth):
                    rim = source[tile(slot, layer), edge : edge + 1]
                    if step:
                        rim = rim + LINK * recv_x[step - 1, face, k, layer : layer + 1]
                    send_x[step, face, k, layer : layer + 1] = rim

    def pack_y(step, source):
        for face in range(2, 4):
            edge = 0 if face == 2 else cols - 1
            packed = zero
            for k in range(SHARED):
                slot = tab[32 + face * SHARED + k]
                for layer in range(depth):
                    place = k * depth + layer
                    moved = pltpu.roll(source[tile(slot, layer)], (place - edge) % cols, 1)
                    packed = jnp.where(col == place, moved, packed)
            if step:
                packed = packed + LINK * recv_y[step - 1, face - 2]
            send_y[step, face - 2] = packed

    def unpack(step):
        for face in range(2):
            edge = 0 if face == 0 else rows - 1
            for k in range(SHARED):
                for layer in range(depth):
                    at = tile(face * SHARED + k, layer)
                    halo[at, edge : edge + 1] = LINK * recv_x[step, face, k, layer : layer + 1]
        for face in range(2, 4):
            edge = 0 if face == 2 else cols - 1
            packed = LINK * recv_y[step, face - 2]
            for k in range(SHARED):
                for layer in range(depth):
                    place = k * depth + layer
                    moved = pltpu.roll(packed, (edge - place) % cols, 1)
                    halo[tile(face * SHARED + k, layer)] = jnp.where(col == edge, moved, 0.0)

    def totals(step):
        def body(slot, sums):
            held = tab[slot]
            out_sums = []
            for layer in range(depth):
                at = tile(slot, layer)
                value = field[at] if step == 0 else local[at] + halo[tile(held, layer)]
                if step:
                    field[at] = value
                out_sums.append(sums[layer] + value * value)
            return tuple(out_sums)

        return lax.fori_loop(0, slots, body, (zero,) * depth)

    def update(sums):
        coefs = tuple(SELF - TOTAL * s for s in sums)
        below, above = planes[0], planes[1]

        def body(slot, carry):
            grain = tab[64 + slot]
            values = [field[tile(slot, layer)] for layer in range(depth)]
            small = [LINK * v for v in values]
            low = jnp.where(below == grain, LINK, 0.0)
            high = jnp.where(above == grain, LINK, 0.0)
            for layer in range(depth):
                v, w = values[layer], small[layer]
                near = (
                    jnp.where(row == rows - 1, 0.0, pltpu.roll(w, rows - 1, 0))
                    + jnp.where(row == 0, 0.0, pltpu.roll(w, 1, 0))
                    + jnp.where(col == cols - 1, 0.0, pltpu.roll(w, cols - 1, 1))
                    + jnp.where(col == 0, 0.0, pltpu.roll(w, 1, 1))
                    + (small[layer - 1] if layer else low)
                    + (small[layer + 1] if layer < depth - 1 else high)
                )
                local[tile(slot, layer)] = v * (coefs[layer] + v * w) + near
            return carry

        lax.fori_loop(0, slots, body, 0)

    load.wait()
    pack_x(0, field)
    pl.semaphore_wait(barrier, FACES)
    for step in range(STEPS):
        if step:
            for face in range(FACES):
                arrival(step - 1, face).wait_recv()
            pack_x(step, local)
        copy(step, 0).start()
        copy(step, 1).start()
        pack_y(step, local if step else field)
        copy(step, 2).start()
        copy(step, 3).start()
        if step:
            unpack(step - 1)
        update(totals(step))
    for face in range(FACES):
        arrival(STEPS - 1, face).wait_recv()
    unpack(STEPS - 1)

    def finish(slot, carry):
        held = tab[slot]
        for layer in range(depth):
            at = tile(slot, layer)
            out[at] = local[at] + halo[tile(held, layer)]
        return carry

    lax.fori_loop(0, slots, finish, 0)
    for step in range(STEPS):
        for face in range(FACES):
            copy(step, face).wait_send()


def tables(grain_ids, channel_maps):
    slots = grain_ids.shape[-1]
    maps = channel_maps[0, 0]
    own = jnp.arange(slots, dtype=jnp.int32)
    upper = (jnp.arange(FACES, dtype=jnp.int32) % 2 == 1)[:, None]
    linked = maps >= 0
    key = jnp.where(linked, jnp.where(upper, own[None, :], maps), slots)
    rank = jnp.sum((key[:, None, :] < key[:, :, None]).astype(jnp.int32), axis=2)
    pair = jnp.arange(FACES, dtype=jnp.int32)[:, None] * SHARED + rank
    held = jnp.min(jnp.where(linked, pair, FACES * SHARED), axis=0)
    places = jnp.arange(FACES * SHARED, dtype=jnp.int32)
    source = jnp.sum(jnp.where(held[None, :] == places[:, None], own[None, :], 0), axis=1)
    grains = jnp.where(grain_ids[0, 0] >= 0, grain_ids[0, 0], -1)
    pad = lambda x: jnp.pad(x, (0, 32 - slots))
    return jnp.concatenate([pad(held), pad(source), pad(grains)]).astype(jnp.int32)


def solution(mesh):
    nx, ny = mesh.shape["gx"], mesh.shape["gy"]

    def on_device(order_params, grain_ids, channel_maps, zplanes):
        slots, depth, rows, cols = order_params.shape
        tiles = (slots * depth, rows, cols)
        tab = tables(grain_ids, channel_maps)
        result = pl.pallas_call(
            functools.partial(kernel, slots, depth, nx, ny),
            out_shape=jax.ShapeDtypeStruct(tiles, jnp.float32),
            in_specs=[
                pl.BlockSpec(memory_space=pltpu.SMEM),
                pl.BlockSpec(memory_space=pltpu.VMEM),
                pl.BlockSpec(memory_space=pl.ANY),
            ],
            out_specs=pl.BlockSpec(memory_space=pltpu.VMEM),
            scratch_shapes=[
                pltpu.VMEM(tiles, jnp.float32),
                pltpu.VMEM(tiles, jnp.float32),
                pltpu.VMEM(((slots + 1) * depth, rows, cols), jnp.float32),
                pltpu.VMEM((STEPS, 2, SHARED, depth, cols), jnp.float32),
                pltpu.VMEM((STEPS, 2, SHARED, depth, cols), jnp.float32),
                pltpu.VMEM((STEPS, 2, rows, cols), jnp.float32),
                pltpu.VMEM((STEPS, 2, rows, cols), jnp.float32),
                pltpu.SemaphoreType.DMA,
                pltpu.SemaphoreType.DMA((STEPS, FACES)),
                pltpu.SemaphoreType.DMA((STEPS, FACES)),
            ],
            compiler_params=pltpu.CompilerParams(
                collective_id=0, has_side_effects=True, vmem_limit_bytes=16 * 2**20
            ),
        )(tab, zplanes, order_params.reshape(tiles))
        return result.reshape(order_params.shape)

    in_specs = (
        P(None, None, "gx", "gy"),
        P("gx", "gy", None),
        P("gx", "gy", None, None),
        P(None, "gx", "gy"),
    )
    return jax.shard_map(
        on_device, mesh=mesh, in_specs=in_specs, out_specs=P(None, None, "gx", "gy"), check_vma=False
    )
```

```python
import functools

import jax
import jax.numpy as jnp
from jax import lax
from jax.experimental import pallas as pl
from jax.experimental.pallas import tpu as pltpu
from jax.sharding import PartitionSpec as P

SHARED = 6
FACES = 4
MESH = pl.DeviceIdType.MESH

SELF = 0.45
TOTAL = 0.15
LINK = 0.1

RIM, LOCAL, SUMS = 0, 1, 2


def kernel(slots, depth, nx, ny, maps_in, grains_in, planes_in, start, out, field, local, halo, maps, key_box, table, tab,
           grains, planes, rim_x, got_rim_x, loc_x, got_loc_x, sum_x, got_sum_x, rim_y, got_rim_y, loc_y, got_loc_y, sum_y,
           got_sum_y, next_x, next_y, load_sem, send_sem, recv_sem):
    rows, cols = 8, 128
    i, j = lax.axis_index("gx"), lax.axis_index("gy")
    across = (
        (lax.rem(i + nx - 1, nx), j),
        (lax.rem(i + 1, nx), j),
        (i, lax.rem(j + ny - 1, ny)),
        (i, lax.rem(j + 1, ny)),
    )
    barrier = pltpu.get_barrier_semaphore()
    for device in across:
        pl.semaphore_signal(barrier, inc=1, device_id=device, device_id_type=MESH)
    loads = [
        pltpu.make_async_copy(maps_in, maps, load_sem.at[0]),
        pltpu.make_async_copy(start, field, load_sem.at[1]),
        pltpu.make_async_copy(grains_in, grains, load_sem.at[2]),
        pltpu.make_async_copy(planes_in, planes, load_sem.at[3]),
    ]
    for load in loads:
        load.start()

    row = lax.broadcasted_iota(jnp.int32, (rows, cols), 0)
    col = lax.broadcasted_iota(jnp.int32, (rows, cols), 1)
    zero = jnp.zeros((rows, cols), jnp.float32)

    def tile(slot, layer):
        return slot * depth + layer

    def clear(slot, carry):
        for layer in range(depth):
            halo[tile(slot, layer)] = zero
        return carry

    lax.fori_loop(0, slots + 1, clear, 0)

    loads[0].wait()
    key_box[...] = jnp.full((rows, cols), -1, jnp.int32)
    key_box[0:FACES, 0:slots] = maps[...]
    entries = key_box[...]
    linked = entries >= 0
    upper = (row == 1) | (row == 3)
    key = jnp.where(linked, jnp.where(upper, col, entries), slots)
    rank = jnp.zeros((rows, cols), jnp.int32)
    for slot in range(slots):
        rank = rank + jnp.where(key[:, slot : slot + 1] < key, 1, 0)
    pair = jnp.where(linked & (rank < SHARED), row * SHARED + rank, FACES * SHARED)
    held = jnp.broadcast_to(jnp.min(pair, axis=0, keepdims=True), (rows, cols))
    source = jnp.zeros((rows, cols), jnp.int32)
    for slot in range(slots):
        source = jnp.maximum(source, jnp.where(held[:, slot : slot + 1] == col, slot, 0))
    table[...] = jnp.where(row == 0, held, source)
    fetch = pltpu.make_async_copy(table, tab, load_sem.at[4])
    fetch.start()

    buffers = {
        RIM: ((rim_x, got_rim_x), (rim_y, got_rim_y)),
        LOCAL: ((loc_x, got_loc_x), (loc_y, got_loc_y)),
        SUMS: ((sum_x, got_sum_x), (sum_y, got_sum_y)),
    }

    def copy(kind, face):
        sent, got = buffers[kind][face // 2]
        return pltpu.make_async_remote_copy(
            src_ref=sent.at[face % 2],
            dst_ref=got.at[1 - face % 2],
            send_sem=send_sem.at[kind, face],
            recv_sem=recv_sem.at[kind, face ^ 1],
            device_id=across[face],
            device_id_type=MESH,
        )

    def wait_for(kind, face):
        copy(kind, face ^ 1).wait_recv()

    def pair_slot(face, k):
        return tab[1, face * SHARED + k]

    def gather_columns(face, column, tiles):
        packed = zero
        for k in range(SHARED):
            slot = pair_slot(face, k)
            for layer in range(depth):
                place = k * depth + layer
                moved = pltpu.roll(tiles[tile(slot, layer)], (place - column) % cols, 1)
                packed = jnp.where(col == place, moved, packed)
        return packed

    def scatter(face, layer_row, packed):
        edge = 0 if face % 2 == 0 else (rows if face < 2 else cols) - 1
        for k in range(SHARED):
            for layer in range(depth):
                at = tile(face * SHARED + k, layer)
                if face < 2:
                    halo[at, edge : edge + 1] = LINK * layer_row(layer, k)
                else:
                    moved = pltpu.roll(packed, (edge - (k * depth + layer)) % cols, 1)
                    halo[at] = jnp.where(col == edge, moved, 0.0)

    def totals(first):
        def body(slot, sums):
            held_pair = tab[0, slot]
            out_sums = []
            for layer in range(depth):
                at = tile(slot, layer)
                value = field[at] if first else local[at] + halo[tile(held_pair, layer)]
                if not first:
                    field[at] = value
                out_sums.append(sums[layer] + value * value)
            return tuple(out_sums)

        return lax.fori_loop(0, slots, body, (zero,) * depth)

    def update(sums):
        coefs = tuple(SELF - TOTAL * s for s in sums)
        below, above = planes[0], planes[1]

        def body(slot, carry):
            grain = grains[slot]
            grain = jnp.where(grain >= 0, grain, -1)
            values = [field[tile(slot, layer)] for layer in range(depth)]
            small = [LINK * v for v in values]
            low = jnp.where(below == grain, LINK, 0.0)
            high = jnp.where(above == grain, LINK, 0.0)
            for layer in range(depth):
                v, w = values[layer], small[layer]
                near = (
                    jnp.where(row == rows - 1, 0.0, pltpu.roll(w, rows - 1, 0))
                    + jnp.where(row == 0, 0.0, pltpu.roll(w, 1, 0))
                    + jnp.where(col == cols - 1, 0.0, pltpu.roll(w, cols - 1, 1))
                    + jnp.where(col == 0, 0.0, pltpu.roll(w, 1, 1))
                    + (small[layer - 1] if layer else low)
                    + (small[layer + 1] if layer < depth - 1 else high)
                )
                local[tile(slot, layer)] = v * (coefs[layer] + v * w) + near
            return carry

        lax.fori_loop(0, slots, body, 0)

    loads[1].wait()
    sums = totals(True)
    fetch.wait()
    for face in range(2):
        edge = 0 if face == 0 else rows - 1
        for k in range(SHARED):
            slot = pair_slot(face, k)
            for layer in range(depth):
                rim_x[face, layer, k : k + 1] = field[tile(slot, layer), edge : edge + 1]
    for face in range(2, 4):
        rim_y[face - 2] = gather_columns(face, 0 if face == 2 else cols - 1, field)
    pl.semaphore_wait(barrier, FACES)
    for face in range(FACES):
        copy(RIM, face).start()

    loads[2].wait()
    loads[3].wait()
    update(sums)

    for face in range(2):
        edge, second = (0, 1) if face == 0 else (rows - 1, rows - 2)
        for k in range(SHARED):
            slot = pair_slot(face, k)
            grain = grains[slot]
            grain = jnp.where(grain >= 0, grain, -1)
            for layer in range(depth):
                at = tile(slot, layer)
                loc_x[face, 0, layer, k : k + 1] = local[at, edge : edge + 1]
                behind = local[at, second : second + 1]
                if layer == 0:
                    behind = behind + jnp.where(planes[0, edge : edge + 1] == grain, 1.0, 0.0)
                if layer == depth - 1:
                    behind = behind + jnp.where(planes[1, edge : edge + 1] == grain, 1.0, 0.0)
                loc_x[face, 1, layer, k : k + 1] = behind
    for face in range(2, 4):
        edge, second = (0, 1) if face == 2 else (cols - 1, cols - 2)
        loc_y[face - 2, 0] = gather_columns(face, edge, local)
        behind = gather_columns(face, second, local)
        for k in range(SHARED):
            grain = grains[pair_slot(face, k)]
            grain = jnp.where(grain >= 0, grain, -1)
            for plane, layer in ((0, 0), (1, depth - 1)):
                place = k * depth + layer
                frozen = jnp.where(planes[plane] == grain, 1.0, 0.0)
                moved = pltpu.roll(frozen, (place - edge) % cols, 1)
                behind = behind + jnp.where(col == place, moved, 0.0)
        loc_y[face - 2, 1] = behind
    for face in range(FACES):
        copy(LOCAL, face).start()

    for face in range(FACES):
        wait_for(RIM, face)
        if face < 2:
            scatter(face, lambda layer, k: got_rim_x[face, layer, k : k + 1], None)
        else:
            scatter(face, None, LINK * got_rim_y[face - 2])
    sums = totals(False)

    for face in range(2):
        edge = 0 if face == 0 else rows - 1
        for layer in range(depth):
            sum_x[face, layer : layer + 1] = sums[layer][edge : edge + 1]
    for face in range(2, 4):
        edge = 0 if face == 2 else cols - 1
        packed = zero
        for layer in range(depth):
            packed = jnp.where(col == layer, pltpu.roll(sums[layer], (layer - edge) % cols, 1), packed)
        two = packed + pltpu.roll(packed, depth, 1)
        four = two + pltpu.roll(two, 2 * depth, 1)
        sum_y[face - 2] = four + pltpu.roll(two, 4 * depth, 1)
    for face in range(FACES):
        copy(SUMS, face).start()

    update(sums)

    for face in range(FACES):
        wait_for(LOCAL, face)
        if face < 2:
            for layer in range(depth):
                next_x[face, layer] = got_loc_x[face, 0, layer] + LINK * rim_x[face, layer]
            scatter(face, lambda layer, k: next_x[face, layer, k : k + 1], None)
        else:
            next_y[face - 2] = got_loc_y[face - 2, 0] + LINK * rim_y[face - 2]
            scatter(face, None, LINK * next_y[face - 2])
    update(totals(False))

    group = lax.rem(col, depth)
    lane = col[:SHARED]
    for face in range(FACES):
        wait_for(SUMS, face)
        if face < 2:
            rims = [next_x[face, layer] for layer in range(depth)]
            for layer in range(depth):
                r = rims[layer]
                near = (
                    got_loc_x[face, 1, layer]
                    + loc_x[face, 0, layer]
                    + LINK * got_rim_x[face, layer]
                    + jnp.where(lane == cols - 1, 0.0, pltpu.roll(r, cols - 1, 1))
                    + jnp.where(lane == 0, 0.0, pltpu.roll(r, 1, 1))
                )
                if layer:
                    near = near + rims[layer - 1]
                if layer < depth - 1:
                    near = near + rims[layer + 1]
                total = jnp.broadcast_to(got_sum_x[face, layer : layer + 1], r.shape)
                next_x[face, layer] = r * (SELF - TOTAL * total + LINK * r * r) + LINK * near
            scatter(face, lambda layer, k: next_x[face, layer, k : k + 1], None)
        else:
            r = next_y[face - 2]
            near = (
                got_loc_y[face - 2, 1]
                + loc_y[face - 2, 0]
                + LINK * got_rim_y[face - 2]
                + jnp.where(row == rows - 1, 0.0, pltpu.roll(r, rows - 1, 0))
                + jnp.where(row == 0, 0.0, pltpu.roll(r, 1, 0))
                + jnp.where(group == depth - 1, 0.0, pltpu.roll(r, cols - 1, 1))
                + jnp.where(group == 0, 0.0, pltpu.roll(r, 1, 1))
            )
            total = got_sum_y[face - 2]
            scatter(face, None, LINK * (r * (SELF - TOTAL * total + LINK * r * r) + LINK * near))

    def finish(slot, carry):
        held_pair = tab[0, slot]
        for layer in range(depth):
            at = tile(slot, layer)
            out[at] = local[at] + halo[tile(held_pair, layer)]
        return carry

    lax.fori_loop(0, slots, finish, 0)
    for kind in (RIM, LOCAL, SUMS):
        for face in range(FACES):
            copy(kind, face).wait_send()


def solution(mesh):
    nx, ny = mesh.shape["gx"], mesh.shape["gy"]

    def on_device(order_params, grain_ids, channel_maps, zplanes):
        slots, depth, rows, cols = order_params.shape
        tiles = (slots * depth, rows, cols)
        rim_x = pltpu.VMEM((2, depth, SHARED, cols), jnp.float32)
        loc_x = pltpu.VMEM((2, 2, depth, SHARED, cols), jnp.float32)
        sum_x = pltpu.VMEM((2, depth, cols), jnp.float32)
        rim_y = pltpu.VMEM((2, rows, cols), jnp.float32)
        loc_y = pltpu.VMEM((2, 2, rows, cols), jnp.float32)
        operands = (channel_maps.reshape(FACES, slots), grain_ids.reshape(slots), zplanes, order_params.reshape(tiles))
        result = pl.pallas_call(
            functools.partial(kernel, slots, depth, nx, ny),
            out_shape=jax.ShapeDtypeStruct(tiles, jnp.float32),
            in_specs=[pl.BlockSpec(memory_space=pltpu.HBM)] * 4,
            out_specs=pl.BlockSpec(memory_space=pltpu.VMEM),
            scratch_shapes=[
                pltpu.VMEM(tiles, jnp.float32),
                pltpu.VMEM(tiles, jnp.float32),
                pltpu.VMEM(((FACES * SHARED + 1) * depth, rows, cols), jnp.float32),
                pltpu.VMEM((FACES, slots), jnp.int32),
                pltpu.VMEM((rows, cols), jnp.int32),
                pltpu.VMEM((rows, cols), jnp.int32),
                pltpu.SMEM((rows, cols), jnp.int32),
                pltpu.SMEM((slots,), jnp.int32),
                pltpu.VMEM((2, rows, cols), jnp.int32),
                rim_x, rim_x, loc_x, loc_x, sum_x, sum_x,
                rim_y, rim_y, loc_y, loc_y, rim_y, rim_y,
                rim_x, rim_y,
                pltpu.SemaphoreType.DMA((5,)),
                pltpu.SemaphoreType.DMA((3, FACES)),
                pltpu.SemaphoreType.DMA((3, FACES)),
            ],
            compiler_params=pltpu.CompilerParams(
                collective_id=0, has_side_effects=True, vmem_limit_bytes=16 * 2**20
            ),
        )(*[pltpu.with_memory_space_constraint(x, pltpu.HBM) for x in operands])
        return result.reshape(order_params.shape)

    in_specs = (
        P(None, None, "gx", "gy"),
        P("gx", "gy", None),
        P("gx", "gy", None, None),
        P(None, "gx", "gy"),
    )
    return jax.shard_map(
        on_device, mesh=mesh, in_specs=in_specs, out_specs=P(None, None, "gx", "gy"), check_vma=False
    )
```

```python
import functools

import jax
import jax.numpy as jnp
from jax import lax
from jax.experimental import pallas as pl
from jax.experimental.pallas import tpu as pltpu
from jax.sharding import PartitionSpec as P

SHARED = 6
FACES = 4
MESH = pl.DeviceIdType.MESH

SELF = 0.45
TOTAL = 0.15
LINK = 0.1

RIM, LOCAL, BEHIND, SUMS = 0, 1, 2, 3
UNROLL = 8


def kernel(slots, depth, nx, ny, maps_in, grains_in, planes_in, start, out, field, local, halo, maps, key_box, table, tab,
           grains, planes, rim_x, got_rim_x, loc_x, got_loc_x, row_x, got_row_x, sum_x, got_sum_x, rim_y, got_rim_y, loc_y,
           got_loc_y, row_y, got_row_y, sum_y, got_sum_y, next_x, next_y, load_sem, send_sem, recv_sem):
    rows, cols = 8, 128
    i, j = lax.axis_index("gx"), lax.axis_index("gy")
    across = (
        (lax.rem(i + nx - 1, nx), j),
        (lax.rem(i + 1, nx), j),
        (i, lax.rem(j + ny - 1, ny)),
        (i, lax.rem(j + 1, ny)),
    )
    barrier = pltpu.get_barrier_semaphore()
    for device in across:
        pl.semaphore_signal(barrier, inc=1, device_id=device, device_id_type=MESH)
    loads = [
        pltpu.make_async_copy(maps_in, maps, load_sem.at[0]),
        pltpu.make_async_copy(start, field.at[pl.ds(0, slots * depth)], load_sem.at[1]),
        pltpu.make_async_copy(grains_in, grains, load_sem.at[2]),
        pltpu.make_async_copy(planes_in, planes, load_sem.at[3]),
    ]
    for load in loads:
        load.start()

    row = lax.broadcasted_iota(jnp.int32, (rows, cols), 0)
    col = lax.broadcasted_iota(jnp.int32, (rows, cols), 1)
    zero = jnp.zeros((rows, cols), jnp.float32)

    def tile(slot, layer):
        return slot * depth + layer

    def clear(slot, carry):
        for layer in range(depth):
            halo[tile(slot, layer)] = zero
        return carry

    lax.fori_loop(0, slots + 1, clear, 0)
    for layer in range(depth):
        field[tile(slots, layer)] = zero
        local[tile(slots, layer)] = zero

    loads[0].wait()
    key_box[...] = jnp.full((rows, cols), -1, jnp.int32)
    key_box[0:FACES, 0:slots] = maps[...]
    entries = key_box[...]
    linked = entries >= 0
    upper = (row == 1) | (row == 3)
    key = jnp.where(linked, jnp.where(upper, col, entries), slots)
    rank = jnp.zeros((rows, cols), jnp.int32)
    for slot in range(slots):
        rank = rank + jnp.where(key[:, slot : slot + 1] < key, 1, 0)
    pair = jnp.where(linked & (rank < SHARED), row * SHARED + rank, FACES * SHARED)
    held = jnp.broadcast_to(jnp.min(pair, axis=0, keepdims=True), (rows, cols))
    source = jnp.full((rows, cols), slots, jnp.int32)
    for slot in range(slots):
        source = jnp.minimum(source, jnp.where(held[:, slot : slot + 1] == col, slot, slots))
    table[...] = jnp.where(row == 0, held, source)
    fetch = pltpu.make_async_copy(table, tab, load_sem.at[4])
    fetch.start()

    buffers = {
        RIM: ((rim_x, got_rim_x), (rim_y, got_rim_y)),
        LOCAL: ((loc_x, got_loc_x), (loc_y, got_loc_y)),
        BEHIND: ((row_x, got_row_x), (row_y, got_row_y)),
        SUMS: ((sum_x, got_sum_x), (sum_y, got_sum_y)),
    }

    def copy(kind, face):
        sent, got = buffers[kind][face // 2]
        return pltpu.make_async_remote_copy(
            src_ref=sent.at[face % 2],
            dst_ref=got.at[1 - face % 2],
            send_sem=send_sem.at[kind, face],
            recv_sem=recv_sem.at[kind, face ^ 1],
            device_id=across[face],
            device_id_type=MESH,
        )

    def wait_for(kind, face):
        copy(kind, face ^ 1).wait_recv()

    def pair_slot(face, k):
        return tab[1, face * SHARED + k]

    def grain_of(slot):
        grain = grains[jnp.minimum(slot, slots - 1)]
        return jnp.where(grain >= 0, grain, -1)

    def gather_columns(face, column, tiles):
        packed = zero
        for k in range(SHARED):
            slot = pair_slot(face, k)
            for layer in range(depth):
                place = k * depth + layer
                moved = pltpu.roll(tiles[tile(slot, layer)], (place - column) % cols, 1)
                packed = jnp.where(col == place, moved, packed)
        return packed

    def scatter(face, layer_row, packed):
        edge = 0 if face % 2 == 0 else (rows if face < 2 else cols) - 1
        for k in range(SHARED):
            for layer in range(depth):
                at = tile(face * SHARED + k, layer)
                if face < 2:
                    halo[at, edge : edge + 1] = LINK * layer_row(layer, k)
                else:
                    moved = pltpu.roll(packed, (edge - (k * depth + layer)) % cols, 1)
                    halo[at] = jnp.where(col == edge, moved, 0.0)

    def totals(first, keep=True):
        def body(slot, sums):
            held_pair = tab[0, slot]
            out_sums = []
            for layer in range(depth):
                at = tile(slot, layer)
                value = field[at] if first else local[at] + halo[tile(held_pair, layer)]
                if not first and keep:
                    field[at] = value
                out_sums.append(sums[layer] + value * value)
            return tuple(out_sums)

        return lax.fori_loop(0, slots, body, (zero,) * depth, unroll=UNROLL)

    def update(sums):
        coefs = tuple(SELF - TOTAL * s for s in sums)
        below, above = planes[0], planes[1]

        def body(slot, carry):
            grain = grain_of(slot)
            values = [field[tile(slot, layer)] for layer in range(depth)]
            small = [LINK * v for v in values]
            low = jnp.where(below == grain, LINK, 0.0)
            high = jnp.where(above == grain, LINK, 0.0)
            for layer in range(depth):
                v, w = values[layer], small[layer]
                near = (
                    jnp.where(row == rows - 1, 0.0, pltpu.roll(w, rows - 1, 0))
                    + jnp.where(row == 0, 0.0, pltpu.roll(w, 1, 0))
                    + jnp.where(col == cols - 1, 0.0, pltpu.roll(w, cols - 1, 1))
                    + jnp.where(col == 0, 0.0, pltpu.roll(w, 1, 1))
                    + (small[layer - 1] if layer else low)
                    + (small[layer + 1] if layer < depth - 1 else high)
                )
                local[tile(slot, layer)] = v * (coefs[layer] + v * w) + near
            return carry

        lax.fori_loop(0, slots, body, 0, unroll=UNROLL)

    loads[1].wait()
    sums = totals(True)
    fetch.wait()
    for face in range(2):
        edge = 0 if face == 0 else rows - 1
        for k in range(SHARED):
            slot = pair_slot(face, k)
            for layer in range(depth):
                rim_x[face, layer, k : k + 1] = field[tile(slot, layer), edge : edge + 1]
    for face in range(2, 4):
        rim_y[face - 2] = gather_columns(face, 0 if face == 2 else cols - 1, field)
    pl.semaphore_wait(barrier, FACES)
    for face in range(FACES):
        copy(RIM, face).start()

    loads[2].wait()
    loads[3].wait()
    update(sums)

    for face in range(2):
        edge = 0 if face == 0 else rows - 1
        for k in range(SHARED):
            slot = pair_slot(face, k)
            for layer in range(depth):
                loc_x[face, layer, k : k + 1] = local[tile(slot, layer), edge : edge + 1]
        copy(LOCAL, face).start()
    for face in range(2, 4):
        loc_y[face - 2] = gather_columns(face, 0 if face == 2 else cols - 1, local)
        copy(LOCAL, face).start()

    for face in range(2):
        edge, second = (0, 1) if face == 0 else (rows - 1, rows - 2)
        for k in range(SHARED):
            slot = pair_slot(face, k)
            grain = grain_of(slot)
            for layer in range(depth):
                behind = local[tile(slot, layer), second : second + 1]
                if layer == 0:
                    behind = behind + jnp.where(planes[0, edge : edge + 1] == grain, 1.0, 0.0)
                if layer == depth - 1:
                    behind = behind + jnp.where(planes[1, edge : edge + 1] == grain, 1.0, 0.0)
                row_x[face, layer, k : k + 1] = behind
        copy(BEHIND, face).start()
    for face in range(2, 4):
        edge, second = (0, 1) if face == 2 else (cols - 1, cols - 2)
        behind = gather_columns(face, second, local)
        for k in range(SHARED):
            grain = grain_of(pair_slot(face, k))
            for plane, layer in ((0, 0), (1, depth - 1)):
                place = k * depth + layer
                frozen = jnp.where(planes[plane] == grain, 1.0, 0.0)
                moved = pltpu.roll(frozen, (place - edge) % cols, 1)
                behind = behind + jnp.where(col == place, moved, 0.0)
        row_y[face - 2] = behind
        copy(BEHIND, face).start()

    for face in range(2, 4):
        wait_for(RIM, face)
        scatter(face, None, LINK * got_rim_y[face - 2])
    sums = totals(False, keep=False)
    for face in range(2):
        edge = 0 if face == 0 else rows - 1
        for layer in range(depth):
            across_it = loc_x[face, layer]
            across_it = jnp.sum(across_it * across_it, axis=0, keepdims=True)
            sum_x[face, layer : layer + 1] = sums[layer][edge : edge + 1] - across_it
        copy(SUMS, face).start()

    for face in range(2):
        wait_for(RIM, face)
        scatter(face, lambda layer, k: got_rim_x[face, layer, k : k + 1], None)
    sums = totals(False)
    for face in range(2, 4):
        edge = 0 if face == 2 else cols - 1
        packed = zero
        for layer in range(depth):
            packed = jnp.where(col == layer, pltpu.roll(sums[layer], (layer - edge) % cols, 1), packed)
        two = packed + pltpu.roll(packed, depth, 1)
        four = two + pltpu.roll(two, 2 * depth, 1)
        sum_y[face - 2] = four + pltpu.roll(two, 4 * depth, 1)
        copy(SUMS, face).start()

    update(sums)

    for face in range(FACES):
        wait_for(LOCAL, face)
        if face < 2:
            for layer in range(depth):
                next_x[face, layer] = got_loc_x[face, layer] + LINK * rim_x[face, layer]
            scatter(face, lambda layer, k: next_x[face, layer, k : k + 1], None)
        else:
            next_y[face - 2] = got_loc_y[face - 2] + LINK * rim_y[face - 2]
            scatter(face, None, LINK * next_y[face - 2])
    update(totals(False))

    group = lax.rem(col, depth)
    lane = col[:SHARED]
    for face in range(FACES):
        wait_for(BEHIND, face)
        wait_for(SUMS, face)
        if face < 2:
            rims = [next_x[face, layer] for layer in range(depth)]
            for layer in range(depth):
                r = rims[layer]
                near = (
                    got_row_x[face, layer]
                    + loc_x[face, layer]
                    + LINK * got_rim_x[face, layer]
                    + jnp.where(lane == cols - 1, 0.0, pltpu.roll(r, cols - 1, 1))
                    + jnp.where(lane == 0, 0.0, pltpu.roll(r, 1, 1))
                )
                if layer:
                    near = near + rims[layer - 1]
                if layer < depth - 1:
                    near = near + rims[layer + 1]
                total = got_sum_x[face, layer : layer + 1] + jnp.sum(r * r, axis=0, keepdims=True)
                total = jnp.broadcast_to(total, r.shape)
                next_x[face, layer] = r * (SELF - TOTAL * total + LINK * r * r) + LINK * near
            scatter(face, lambda layer, k: next_x[face, layer, k : k + 1], None)
        else:
            r = next_y[face - 2]
            near = (
                got_row_y[face - 2]
                + loc_y[face - 2]
                + LINK * got_rim_y[face - 2]
                + jnp.where(row == rows - 1, 0.0, pltpu.roll(r, rows - 1, 0))
                + jnp.where(row == 0, 0.0, pltpu.roll(r, 1, 0))
                + jnp.where(group == depth - 1, 0.0, pltpu.roll(r, cols - 1, 1))
                + jnp.where(group == 0, 0.0, pltpu.roll(r, 1, 1))
            )
            total = got_sum_y[face - 2]
            scatter(face, None, LINK * (r * (SELF - TOTAL * total + LINK * r * r) + LINK * near))

    def finish(slot, carry):
        held_pair = tab[0, slot]
        for layer in range(depth):
            at = tile(slot, layer)
            out[at] = local[at] + halo[tile(held_pair, layer)]
        return carry

    lax.fori_loop(0, slots, finish, 0)
    for kind in (RIM, LOCAL, BEHIND, SUMS):
        for face in range(FACES):
            copy(kind, face).wait_send()


def solution(mesh):
    nx, ny = mesh.shape["gx"], mesh.shape["gy"]

    def on_device(order_params, grain_ids, channel_maps, zplanes):
        slots, depth, rows, cols = order_params.shape
        tiles = (slots * depth, rows, cols)
        rim_x = pltpu.VMEM((2, depth, SHARED, cols), jnp.float32)
        sum_x = pltpu.VMEM((2, depth, cols), jnp.float32)
        rim_y = pltpu.VMEM((2, rows, cols), jnp.float32)
        operands = (channel_maps.reshape(FACES, slots), grain_ids.reshape(slots), zplanes, order_params.reshape(tiles))
        result = pl.pallas_call(
            functools.partial(kernel, slots, depth, nx, ny),
            out_shape=jax.ShapeDtypeStruct(tiles, jnp.float32),
            in_specs=[pl.BlockSpec(memory_space=pltpu.HBM)] * 4,
            out_specs=pl.BlockSpec(memory_space=pltpu.VMEM),
            scratch_shapes=[
                pltpu.VMEM(((slots + 1) * depth, rows, cols), jnp.float32),
                pltpu.VMEM(((slots + 1) * depth, rows, cols), jnp.float32),
                pltpu.VMEM(((FACES * SHARED + 1) * depth, rows, cols), jnp.float32),
                pltpu.VMEM((FACES, slots), jnp.int32),
                pltpu.VMEM((rows, cols), jnp.int32),
                pltpu.VMEM((rows, cols), jnp.int32),
                pltpu.SMEM((rows, cols), jnp.int32),
                pltpu.SMEM((slots,), jnp.int32),
                pltpu.VMEM((2, rows, cols), jnp.int32),
                rim_x, rim_x, rim_x, rim_x, rim_x, rim_x, sum_x, sum_x,
                rim_y, rim_y, rim_y, rim_y, rim_y, rim_y, rim_y, rim_y,
                rim_x, rim_y,
                pltpu.SemaphoreType.DMA((5,)),
                pltpu.SemaphoreType.DMA((4, FACES)),
                pltpu.SemaphoreType.DMA((4, FACES)),
            ],
            compiler_params=pltpu.CompilerParams(
                collective_id=0, has_side_effects=True, vmem_limit_bytes=16 * 2**20
            ),
        )(*[pltpu.with_memory_space_constraint(x, pltpu.HBM) for x in operands])
        return result.reshape(order_params.shape)

    in_specs = (
        P(None, None, "gx", "gy"),
        P("gx", "gy", None),
        P("gx", "gy", None, None),
        P(None, "gx", "gy"),
    )
    return jax.shard_map(
        on_device, mesh=mesh, in_specs=in_specs, out_specs=P(None, None, "gx", "gy"), check_vma=False
    )
```

```python
import functools

import jax
import jax.numpy as jnp
from jax import lax
from jax.experimental import pallas as pl
from jax.experimental.pallas import tpu as pltpu
from jax.sharding import PartitionSpec as P

SHARED = 6
FACES = 4
MESH = pl.DeviceIdType.MESH

SELF = 0.45
TOTAL = 0.15
LINK = 0.1

RIM, LOCAL, BEHIND, SUMS, CORNER = 0, 1, 2, 3, 4
UNROLL = 8


def kernel(slots, depth, nx, ny, maps_in, grains_in, planes_in, start, out, field, local, halo, halo2, maps, key_box, table, tab,
           grains, planes, rim_x, got_rim_x, loc_x, got_loc_x, row_x, got_row_x, sum_x, got_sum_x, rim_y, got_rim_y, loc_y,
           got_loc_y, row_y, got_row_y, sum_y, got_sum_y, next_x, next_y, cor_y, got_cor_y, got_cor_x, load_sem, send_sem, recv_sem):
    rows, cols = 8, 128
    i, j = lax.axis_index("gx"), lax.axis_index("gy")
    across = (
        (lax.rem(i + nx - 1, nx), j),
        (lax.rem(i + 1, nx), j),
        (i, lax.rem(j + ny - 1, ny)),
        (i, lax.rem(j + 1, ny)),
    )
    barrier = pltpu.get_barrier_semaphore()
    for device in across:
        pl.semaphore_signal(barrier, inc=1, device_id=device, device_id_type=MESH)
    loads = [
        pltpu.make_async_copy(maps_in, maps, load_sem.at[0]),
        pltpu.make_async_copy(start, field.at[pl.ds(0, slots * depth)], load_sem.at[1]),
        pltpu.make_async_copy(grains_in, grains, load_sem.at[2]),
        pltpu.make_async_copy(planes_in, planes, load_sem.at[3]),
    ]
    for load in loads:
        load.start()

    row = lax.broadcasted_iota(jnp.int32, (rows, cols), 0)
    col = lax.broadcasted_iota(jnp.int32, (rows, cols), 1)
    lane = col[:SHARED]
    zero = jnp.zeros((rows, cols), jnp.float32)

    def tile(slot, layer):
        return slot * depth + layer

    def clear(slot, carry):
        for layer in range(depth):
            halo[tile(slot, layer)] = zero
            halo2[tile(slot, layer)] = zero
        return carry

    lax.fori_loop(0, slots + 1, clear, 0)
    for layer in range(depth):
        field[tile(slots, layer)] = zero
        local[tile(slots, layer)] = zero

    loads[0].wait()
    key_box[...] = jnp.full((rows, cols), -1, jnp.int32)
    key_box[0:FACES, 0:slots] = maps[...]
    entries = key_box[...]
    linked = entries >= 0
    upper = (row == 1) | (row == 3)
    key = jnp.where(linked, jnp.where(upper, col, entries), slots)
    rank = jnp.zeros((rows, cols), jnp.int32)
    for slot in range(slots):
        rank = rank + jnp.where(key[:, slot : slot + 1] < key, 1, 0)
    pair = jnp.where(linked & (rank < SHARED), row * SHARED + rank, FACES * SHARED)
    held = jnp.broadcast_to(jnp.min(pair, axis=0, keepdims=True), (rows, cols))
    source = jnp.full((rows, cols), slots, jnp.int32)
    for slot in range(slots):
        source = jnp.minimum(source, jnp.where(held[:, slot : slot + 1] == col, slot, slots))
    table[...] = jnp.where(row == 0, held, source)
    fetch = pltpu.make_async_copy(table, tab, load_sem.at[4])
    fetch.start()

    buffers = {
        RIM: ((rim_x, got_rim_x), (rim_y, got_rim_y)),
        LOCAL: ((loc_x, got_loc_x), (loc_y, got_loc_y)),
        BEHIND: ((row_x, got_row_x), (row_y, got_row_y)),
        SUMS: ((sum_x, got_sum_x), (sum_y, got_sum_y)),
        CORNER: (None, (cor_y, got_cor_y)),
    }

    def copy(kind, face):
        if kind == CORNER and face < 2:
            source, target = got_cor_y.at[:, face], got_cor_x.at[1 - face]
        else:
            sent, got = buffers[kind][face // 2]
            source, target = sent.at[face % 2], got.at[1 - face % 2]
        return pltpu.make_async_remote_copy(
            src_ref=source,
            dst_ref=target,
            send_sem=send_sem.at[kind, face],
            recv_sem=recv_sem.at[kind, face ^ 1],
            device_id=across[face],
            device_id_type=MESH,
        )

    def wait_for(kind, face):
        copy(kind, face ^ 1).wait_recv()

    def pair_slot(face, k):
        return tab[1, face * SHARED + k]

    def grain_of(slot):
        grain = grains[jnp.minimum(slot, slots - 1)]
        return jnp.where(grain >= 0, grain, -1)

    def gather_columns(face, column, tiles):
        packed = zero
        for k in range(SHARED):
            slot = pair_slot(face, k)
            for layer in range(depth):
                place = k * depth + layer
                moved = pltpu.roll(tiles[tile(slot, layer)], (place - column) % cols, 1)
                packed = jnp.where(col == place, moved, packed)
        return packed

    def corners(rims, column):
        packed = jnp.zeros((SHARED, cols), jnp.float32)
        for layer in range(depth):
            packed = jnp.where(lane == layer, pltpu.roll(rims[layer], (layer - column) % cols, 1), packed)
        return packed

    def per_pair(layers):
        two = layers + pltpu.roll(layers, depth, 1)
        four = two + pltpu.roll(two, 2 * depth, 1)
        return four + pltpu.roll(two, 4 * depth, 1)

    def scatter(face, layer_row, packed, halo=halo):
        edge = 0 if face % 2 == 0 else (rows if face < 2 else cols) - 1
        for k in range(SHARED):
            for layer in range(depth):
                at = tile(face * SHARED + k, layer)
                if face < 2:
                    halo[at, edge : edge + 1] = LINK * layer_row(layer, k)
                else:
                    moved = pltpu.roll(packed, (edge - (k * depth + layer)) % cols, 1)
                    halo[at] = jnp.where(col == edge, moved, 0.0)

    def totals(first, halo=halo, keep=True):
        def body(slot, sums):
            held_pair = tab[0, slot]
            out_sums = []
            for layer in range(depth):
                at = tile(slot, layer)
                value = field[at] if first else local[at] + halo[tile(held_pair, layer)]
                if not first and keep:
                    field[at] = value
                out_sums.append(sums[layer] + value * value)
            return tuple(out_sums)

        return lax.fori_loop(0, slots, body, (zero,) * depth, unroll=UNROLL)

    def update(sums):
        coefs = tuple(SELF - TOTAL * s for s in sums)
        below, above = planes[0], planes[1]

        def body(slot, carry):
            grain = grain_of(slot)
            values = [field[tile(slot, layer)] for layer in range(depth)]
            small = [LINK * v for v in values]
            low = jnp.where(below == grain, LINK, 0.0)
            high = jnp.where(above == grain, LINK, 0.0)
            for layer in range(depth):
                v, w = values[layer], small[layer]
                near = (
                    jnp.where(row == rows - 1, 0.0, pltpu.roll(w, rows - 1, 0))
                    + jnp.where(row == 0, 0.0, pltpu.roll(w, 1, 0))
                    + jnp.where(col == cols - 1, 0.0, pltpu.roll(w, cols - 1, 1))
                    + jnp.where(col == 0, 0.0, pltpu.roll(w, 1, 1))
                    + (small[layer - 1] if layer else low)
                    + (small[layer + 1] if layer < depth - 1 else high)
                )
                local[tile(slot, layer)] = v * (coefs[layer] + v * w) + near
            return carry

        lax.fori_loop(0, slots, body, 0, unroll=UNROLL)

    loads[1].wait()
    sums = totals(True)
    fetch.wait()
    for face in range(2):
        edge = 0 if face == 0 else rows - 1
        for k in range(SHARED):
            slot = pair_slot(face, k)
            for layer in range(depth):
                rim_x[face, layer, k : k + 1] = field[tile(slot, layer), edge : edge + 1]
    for face in range(2, 4):
        rim_y[face - 2] = gather_columns(face, 0 if face == 2 else cols - 1, field)
    pl.semaphore_wait(barrier, FACES)
    for face in range(FACES):
        copy(RIM, face).start()
    for face in range(2, 4):
        for other in range(2):
            rims = [rim_x[other, layer] for layer in range(depth)]
            cor_y[face - 2, other] = corners(rims, 0 if face == 2 else cols - 1)
        copy(CORNER, face).start()

    loads[2].wait()
    loads[3].wait()
    update(sums)

    for face in range(2):
        edge = 0 if face == 0 else rows - 1
        for k in range(SHARED):
            slot = pair_slot(face, k)
            for layer in range(depth):
                loc_x[face, layer, k : k + 1] = local[tile(slot, layer), edge : edge + 1]
        copy(LOCAL, face).start()
    for face in range(2, 4):
        loc_y[face - 2] = gather_columns(face, 0 if face == 2 else cols - 1, local)
        copy(LOCAL, face).start()

    for face in range(2):
        edge, second = (0, 1) if face == 0 else (rows - 1, rows - 2)
        for k in range(SHARED):
            slot = pair_slot(face, k)
            grain = grain_of(slot)
            for layer in range(depth):
                behind = local[tile(slot, layer), second : second + 1]
                if layer == 0:
                    behind = behind + jnp.where(planes[0, edge : edge + 1] == grain, 1.0, 0.0)
                if layer == depth - 1:
                    behind = behind + jnp.where(planes[1, edge : edge + 1] == grain, 1.0, 0.0)
                row_x[face, layer, k : k + 1] = behind
        copy(BEHIND, face).start()
    for face in range(2, 4):
        edge, second = (0, 1) if face == 2 else (cols - 1, cols - 2)
        behind = gather_columns(face, second, local)
        for k in range(SHARED):
            grain = grain_of(pair_slot(face, k))
            for plane, layer in ((0, 0), (1, depth - 1)):
                place = k * depth + layer
                frozen = jnp.where(planes[plane] == grain, 1.0, 0.0)
                moved = pltpu.roll(frozen, (place - edge) % cols, 1)
                behind = behind + jnp.where(col == place, moved, 0.0)
        row_y[face - 2, 0] = behind
        for other in range(2):
            rims = [loc_x[other, layer] for layer in range(depth)]
            row_y[face - 2, 1 + other, 0:SHARED] = corners(rims, edge)
        copy(BEHIND, face).start()

    for face in range(2, 4):
        wait_for(CORNER, face)
    for face in range(2):
        copy(CORNER, face).start()
    for face in range(2, 4):
        wait_for(RIM, face)
        scatter(face, None, LINK * got_rim_y[face - 2])
    sums = totals(False, keep=False)
    for face in range(2):
        edge = 0 if face == 0 else rows - 1
        for layer in range(depth):
            across_it = loc_x[face, layer]
            across_it = jnp.sum(across_it * across_it, axis=0, keepdims=True)
            sum_x[face, layer : layer + 1] = sums[layer][edge : edge + 1] - across_it
        copy(SUMS, face).start()
    for face in range(2, 4):
        edge = 0 if face == 2 else cols - 1
        packed = zero
        for layer in range(depth):
            packed = jnp.where(col == layer, pltpu.roll(sums[layer], (layer - edge) % cols, 1), packed)
        sum_y[face - 2] = per_pair(packed)
        copy(SUMS, face).start()

    for face in range(2, 4):
        wait_for(LOCAL, face)
        next_y[face - 2] = got_loc_y[face - 2] + LINK * rim_y[face - 2]
        scatter(face, None, LINK * next_y[face - 2], halo2)

    for face in range(2):
        wait_for(RIM, face)
        scatter(face, lambda layer, k: got_rim_x[face, layer, k : k + 1], None)
    update(totals(False))

    for face in range(2):
        wait_for(LOCAL, face)
        for layer in range(depth):
            next_x[face, layer] = got_loc_x[face, layer] + LINK * rim_x[face, layer]
        scatter(face, lambda layer, k: next_x[face, layer, k : k + 1], None, halo2)
    update(totals(False, halo2))

    group = lax.rem(col, depth)
    for face in range(2):
        wait_for(CORNER, face)
    for face in range(FACES):
        wait_for(BEHIND, face)
        wait_for(SUMS, face)
        if face < 2:
            rims = [next_x[face, layer] for layer in range(depth)]
            for layer in range(depth):
                r = rims[layer]
                near = (
                    got_row_x[face, layer]
                    + loc_x[face, layer]
                    + LINK * got_rim_x[face, layer]
                    + jnp.where(lane == cols - 1, 0.0, pltpu.roll(r, cols - 1, 1))
                    + jnp.where(lane == 0, 0.0, pltpu.roll(r, 1, 1))
                )
                if layer:
                    near = near + rims[layer - 1]
                if layer < depth - 1:
                    near = near + rims[layer + 1]
                total = got_sum_x[face, layer : layer + 1] + jnp.sum(r * r, axis=0, keepdims=True)
                total = jnp.broadcast_to(total, r.shape)
                next_x[face, layer] = r * (SELF - TOTAL * total + LINK * r * r) + LINK * near
            scatter(face, lambda layer, k: next_x[face, layer, k : k + 1], None)
        else:
            r = next_y[face - 2]
            near = (
                got_row_y[face - 2, 0]
                + loc_y[face - 2]
                + LINK * got_rim_y[face - 2]
                + jnp.where(row == rows - 1, 0.0, pltpu.roll(r, rows - 1, 0))
                + jnp.where(row == 0, 0.0, pltpu.roll(r, 1, 0))
                + jnp.where(group == depth - 1, 0.0, pltpu.roll(r, cols - 1, 1))
                + jnp.where(group == 0, 0.0, pltpu.roll(r, 1, 1))
            )
            total = got_sum_y[face - 2]
            for other in range(2):
                h, g = got_cor_x[other, face - 2], got_row_y[face - 2, 1 + other, 0:SHARED]
                more = jnp.sum(LINK * h * (2.0 * g + LINK * h), axis=0, keepdims=True)
                more = per_pair(jnp.broadcast_to(more, (rows, cols)))
                total = total + jnp.where(row == (0 if other == 0 else rows - 1), more, 0.0)
            scatter(face, None, LINK * (r * (SELF - TOTAL * total + LINK * r * r) + LINK * near))

    def finish(slot, carry):
        held_pair = tab[0, slot]
        for layer in range(depth):
            at = tile(slot, layer)
            out[at] = local[at] + halo[tile(held_pair, layer)]
        return carry

    lax.fori_loop(0, slots, finish, 0)
    for kind in (RIM, LOCAL, BEHIND, SUMS, CORNER):
        for face in range(FACES):
            copy(kind, face).wait_send()


def solution(mesh):
    nx, ny = mesh.shape["gx"], mesh.shape["gy"]

    def on_device(order_params, grain_ids, channel_maps, zplanes):
        slots, depth, rows, cols = order_params.shape
        tiles = (slots * depth, rows, cols)
        rim_x = pltpu.VMEM((2, depth, SHARED, cols), jnp.float32)
        sum_x = pltpu.VMEM((2, depth, cols), jnp.float32)
        rim_y = pltpu.VMEM((2, rows, cols), jnp.float32)
        row_y = pltpu.VMEM((2, 3, rows, cols), jnp.float32)
        corner = pltpu.VMEM((2, 2, SHARED, cols), jnp.float32)
        operands = (channel_maps.reshape(FACES, slots), grain_ids.reshape(slots), zplanes, order_params.reshape(tiles))
        result = pl.pallas_call(
            functools.partial(kernel, slots, depth, nx, ny),
            out_shape=jax.ShapeDtypeStruct(tiles, jnp.float32),
            in_specs=[pl.BlockSpec(memory_space=pltpu.HBM)] * 4,
            out_specs=pl.BlockSpec(memory_space=pltpu.VMEM),
            scratch_shapes=[
                pltpu.VMEM(((slots + 1) * depth, rows, cols), jnp.float32),
                pltpu.VMEM(((slots + 1) * depth, rows, cols), jnp.float32),
                pltpu.VMEM(((FACES * SHARED + 1) * depth, rows, cols), jnp.float32),
                pltpu.VMEM(((FACES * SHARED + 1) * depth, rows, cols), jnp.float32),
                pltpu.VMEM((FACES, slots), jnp.int32),
                pltpu.VMEM((rows, cols), jnp.int32),
                pltpu.VMEM((rows, cols), jnp.int32),
                pltpu.SMEM((rows, cols), jnp.int32),
                pltpu.SMEM((slots,), jnp.int32),
                pltpu.VMEM((2, rows, cols), jnp.int32),
                rim_x, rim_x, rim_x, rim_x, rim_x, rim_x, sum_x, sum_x,
                rim_y, rim_y, rim_y, rim_y, row_y, row_y, rim_y, rim_y,
                rim_x, rim_y, corner, corner, corner,
                pltpu.SemaphoreType.DMA((5,)),
                pltpu.SemaphoreType.DMA((5, FACES)),
                pltpu.SemaphoreType.DMA((5, FACES)),
            ],
            compiler_params=pltpu.CompilerParams(
                collective_id=0, has_side_effects=True, vmem_limit_bytes=16 * 2**20
            ),
        )(*[pltpu.with_memory_space_constraint(x, pltpu.HBM) for x in operands])
        return result.reshape(order_params.shape)

    in_specs = (
        P(None, None, "gx", "gy"),
        P("gx", "gy", None),
        P("gx", "gy", None, None),
        P(None, "gx", "gy"),
    )
    return jax.shard_map(
        on_device, mesh=mesh, in_specs=in_specs, out_specs=P(None, None, "gx", "gy"), check_vma=False
    )
```

```python
import functools

import jax
import jax.numpy as jnp
from jax import lax
from jax.experimental import pallas as pl
from jax.experimental.pallas import tpu as pltpu
from jax.sharding import PartitionSpec as P

SHARED = 6
FACES = 4
MESH = pl.DeviceIdType.MESH

SELF = 0.45
TOTAL = 0.15
LINK = 0.1

RIM, LOCAL, BEHIND, SUMS, CORNER = 0, 1, 2, 3, 4
UNROLL = 8


def kernel(slots, depth, nx, ny, maps_in, grains_in, planes_in, start, out, field, local, halo, halo2, maps, key_box, table, tab,
           grains, planes, rim_x, got_rim_x, loc_x, got_loc_x, row_x, got_row_x, sum_x, got_sum_x, rim_y, got_rim_y, loc_y,
           got_loc_y, row_y, got_row_y, sum_y, got_sum_y, next_x, next_y, ice_x, cor_y, got_cor_y, got_cor_x, load_sem, send_sem, recv_sem):
    rows, cols = 8, 128
    i, j = lax.axis_index("gx"), lax.axis_index("gy")
    across = (
        (lax.rem(i + nx - 1, nx), j),
        (lax.rem(i + 1, nx), j),
        (i, lax.rem(j + ny - 1, ny)),
        (i, lax.rem(j + 1, ny)),
    )
    barrier = pltpu.get_barrier_semaphore()
    for device in across:
        pl.semaphore_signal(barrier, inc=1, device_id=device, device_id_type=MESH)
    loads = [
        pltpu.make_async_copy(maps_in, maps, load_sem.at[0]),
        pltpu.make_async_copy(start, field.at[pl.ds(0, slots * depth)], load_sem.at[1]),
        pltpu.make_async_copy(grains_in, grains, load_sem.at[2]),
        pltpu.make_async_copy(planes_in, planes, load_sem.at[3]),
    ]
    for load in loads:
        load.start()

    row = lax.broadcasted_iota(jnp.int32, (rows, cols), 0)
    col = lax.broadcasted_iota(jnp.int32, (rows, cols), 1)
    lane = col[:SHARED]
    group = lax.rem(col, depth)
    zero = jnp.zeros((rows, cols), jnp.float32)

    def tile(slot, layer):
        return slot * depth + layer

    def clear(slot, carry):
        for layer in range(depth):
            halo[tile(slot, layer)] = zero
            halo2[tile(slot, layer)] = zero
        return carry

    lax.fori_loop(0, slots + 1, clear, 0)
    for layer in range(depth):
        field[tile(slots, layer)] = zero
        local[tile(slots, layer)] = zero

    loads[0].wait()
    key_box[...] = jnp.full((rows, cols), -1, jnp.int32)
    key_box[0:FACES, 0:slots] = maps[...]
    entries = key_box[...]
    linked = entries >= 0
    upper = (row == 1) | (row == 3)
    key = jnp.where(linked, jnp.where(upper, col, entries), slots)
    rank = jnp.zeros((rows, cols), jnp.int32)
    for slot in range(slots):
        rank = rank + jnp.where(key[:, slot : slot + 1] < key, 1, 0)
    pair = jnp.where(linked & (rank < SHARED), row * SHARED + rank, FACES * SHARED)
    held = jnp.broadcast_to(jnp.min(pair, axis=0, keepdims=True), (rows, cols))
    source = jnp.full((rows, cols), slots, jnp.int32)
    for slot in range(slots):
        source = jnp.minimum(source, jnp.where(held[:, slot : slot + 1] == col, slot, slots))
    table[...] = jnp.where(row == 0, held, source)
    fetch = pltpu.make_async_copy(table, tab, load_sem.at[4])
    fetch.start()

    buffers = {
        RIM: ((rim_x, got_rim_x), (rim_y, got_rim_y)),
        LOCAL: ((loc_x, got_loc_x), (loc_y, got_loc_y)),
        BEHIND: ((row_x, got_row_x), (row_y, got_row_y)),
        SUMS: ((sum_x, got_sum_x), (sum_y, got_sum_y)),
        CORNER: (None, (cor_y, got_cor_y)),
    }

    def copy(kind, face):
        if kind == CORNER and face < 2:
            source, target = got_cor_y.at[:, face], got_cor_x.at[1 - face]
        else:
            sent, got = buffers[kind][face // 2]
            source, target = sent.at[face % 2], got.at[1 - face % 2]
        return pltpu.make_async_remote_copy(
            src_ref=source,
            dst_ref=target,
            send_sem=send_sem.at[kind, face],
            recv_sem=recv_sem.at[kind, face ^ 1],
            device_id=across[face],
            device_id_type=MESH,
        )

    def wait_for(kind, face):
        copy(kind, face ^ 1).wait_recv()

    def pair_slot(face, k):
        return tab[1, face * SHARED + k]

    def grain_of(slot):
        grain = grains[jnp.minimum(slot, slots - 1)]
        return jnp.where((grain >= 0) & (slot < slots), grain, -1)

    def gather_columns(face, column, tiles):
        packed = zero
        for k in range(SHARED):
            slot = pair_slot(face, k)
            for layer in range(depth):
                place = k * depth + layer
                moved = pltpu.roll(tiles[tile(slot, layer)], (place - column) % cols, 1)
                packed = jnp.where(col == place, moved, packed)
        return packed

    def corners(rims, column):
        packed = jnp.zeros((SHARED, cols), jnp.float32)
        for layer in range(depth):
            packed = jnp.where(lane == layer, pltpu.roll(rims[layer], (layer - column) % cols, 1), packed)
        return packed

    def per_pair(layers):
        two = layers + pltpu.roll(layers, depth, 1)
        four = two + pltpu.roll(two, 2 * depth, 1)
        return four + pltpu.roll(two, 4 * depth, 1)

    def columns_of(layers, column):
        packed = zero
        for layer in range(depth):
            packed = jnp.where(col == layer, pltpu.roll(layers[layer], (layer - column) % cols, 1), packed)
        return packed

    def step_x(r, layer, rims, total, beside):
        near = (
            beside
            + jnp.where(lane == cols - 1, 0.0, pltpu.roll(r, cols - 1, 1))
            + jnp.where(lane == 0, 0.0, pltpu.roll(r, 1, 1))
        )
        if layer:
            near = near + rims[layer - 1]
        if layer < depth - 1:
            near = near + rims[layer + 1]
        return r * (SELF - TOTAL * total + LINK * r * r) + LINK * near

    def step_y(r, total, beside):
        near = (
            beside
            + jnp.where(row == rows - 1, 0.0, pltpu.roll(r, rows - 1, 0))
            + jnp.where(row == 0, 0.0, pltpu.roll(r, 1, 0))
            + jnp.where(group == depth - 1, 0.0, pltpu.roll(r, cols - 1, 1))
            + jnp.where(group == 0, 0.0, pltpu.roll(r, 1, 1))
        )
        return r * (SELF - TOTAL * total + LINK * r * r) + LINK * near

    def scatter(face, layer_row, packed, halo=halo):
        edge = 0 if face % 2 == 0 else (rows if face < 2 else cols) - 1
        for k in range(SHARED):
            for layer in range(depth):
                at = tile(face * SHARED + k, layer)
                if face < 2:
                    halo[at, edge : edge + 1] = LINK * layer_row(layer, k)
                else:
                    moved = pltpu.roll(packed, (edge - (k * depth + layer)) % cols, 1)
                    halo[at] = jnp.where(col == edge, moved, 0.0)

    def totals(first, halo=halo, keep=True):
        def body(slot, sums):
            held_pair = tab[0, slot]
            out_sums = []
            for layer in range(depth):
                at = tile(slot, layer)
                value = field[at] if first else local[at] + halo[tile(held_pair, layer)]
                if not first and keep:
                    field[at] = value
                out_sums.append(sums[layer] + value * value)
            return tuple(out_sums)

        return lax.fori_loop(0, slots, body, (zero,) * depth, unroll=UNROLL)

    def update(sums):
        coefs = tuple(SELF - TOTAL * s for s in sums)
        below, above = planes[0], planes[1]

        def body(slot, carry):
            grain = grain_of(slot)
            values = [field[tile(slot, layer)] for layer in range(depth)]
            small = [LINK * v for v in values]
            low = jnp.where(below == grain, LINK, 0.0)
            high = jnp.where(above == grain, LINK, 0.0)
            for layer in range(depth):
                v, w = values[layer], small[layer]
                near = (
                    jnp.where(row == rows - 1, 0.0, pltpu.roll(w, rows - 1, 0))
                    + jnp.where(row == 0, 0.0, pltpu.roll(w, 1, 0))
                    + jnp.where(col == cols - 1, 0.0, pltpu.roll(w, cols - 1, 1))
                    + jnp.where(col == 0, 0.0, pltpu.roll(w, 1, 1))
                    + (small[layer - 1] if layer else low)
                    + (small[layer + 1] if layer < depth - 1 else high)
                )
                local[tile(slot, layer)] = v * (coefs[layer] + v * w) + near
            return carry

        lax.fori_loop(0, slots, body, 0, unroll=slots)

    loads[1].wait()
    sums = totals(True)
    fetch.wait()
    for face in range(2):
        edge = 0 if face == 0 else rows - 1
        for k in range(SHARED):
            slot = pair_slot(face, k)
            for layer in range(depth):
                rim_x[face, layer, k : k + 1] = field[tile(slot, layer), edge : edge + 1]
    for face in range(2, 4):
        rim_y[face - 2] = gather_columns(face, 0 if face == 2 else cols - 1, field)
    pl.semaphore_wait(barrier, FACES)
    for face in range(FACES):
        copy(RIM, face).start()

    loads[2].wait()
    loads[3].wait()
    for face in range(2):
        edge, second = (0, 1) if face == 0 else (rows - 1, rows - 2)
        for k in range(SHARED):
            slot = pair_slot(face, k)
            grain = grain_of(slot)
            for plane in range(2):
                ice_x[face, plane, k : k + 1] = jnp.where(planes[plane, edge : edge + 1] == grain, 1.0, 0.0)
            for layer in range(depth):
                row_x[face, layer, k : k + 1] = field[tile(slot, layer), second : second + 1]
        rims = [rim_x[face, layer] for layer in range(depth)]
        for layer in range(depth):
            beside = row_x[face, layer]
            if layer == 0:
                beside = beside + ice_x[face, 0]
            if layer == depth - 1:
                beside = beside + ice_x[face, 1]
            total = jnp.broadcast_to(sums[layer][edge : edge + 1], beside.shape)
            loc_x[face, layer] = step_x(rims[layer], layer, rims, total, beside)
        copy(LOCAL, face).start()
    ice_y = []
    for face in range(2, 4):
        edge, second = (0, 1) if face == 2 else (cols - 1, cols - 2)
        ice = zero
        for k in range(SHARED):
            grain = grain_of(pair_slot(face, k))
            for plane, layer in ((0, 0), (1, depth - 1)):
                place = k * depth + layer
                frozen = jnp.where(planes[plane] == grain, 1.0, 0.0)
                ice = jnp.where(col == place, pltpu.roll(frozen, (place - edge) % cols, 1), ice)
        ice_y.append(ice)
        total = per_pair(columns_of(sums, edge))
        loc_y[face - 2] = step_y(rim_y[face - 2], total, gather_columns(face, second, field) + ice)
        copy(LOCAL, face).start()
    for face in range(2, 4):
        for other in range(2):
            rims = [rim_x[other, layer] for layer in range(depth)]
            cor_y[face - 2, other] = corners(rims, 0 if face == 2 else cols - 1)
        copy(CORNER, face).start()

    update(sums)

    for face in range(2):
        second = 1 if face == 0 else rows - 2
        for k in range(SHARED):
            slot = pair_slot(face, k)
            for layer in range(depth):
                behind = local[tile(slot, layer), second : second + 1]
                if layer == 0:
                    behind = behind + ice_x[face, 0, k : k + 1]
                if layer == depth - 1:
                    behind = behind + ice_x[face, 1, k : k + 1]
                row_x[face, layer, k : k + 1] = behind
        copy(BEHIND, face).start()
    for face in range(2, 4):
        edge, second = (0, 1) if face == 2 else (cols - 1, cols - 2)
        row_y[face - 2, 0] = gather_columns(face, second, local) + ice_y[face - 2]
        for other in range(2):
            rims = [loc_x[other, layer] for layer in range(depth)]
            row_y[face - 2, 1 + other, 0:SHARED] = corners(rims, edge)
        copy(BEHIND, face).start()

    for face in range(2, 4):
        wait_for(CORNER, face)
    for face in range(2):
        copy(CORNER, face).start()
    for face in range(2, 4):
        wait_for(RIM, face)
        scatter(face, None, LINK * got_rim_y[face - 2])
    sums = totals(False, keep=False)
    for face in range(2):
        edge = 0 if face == 0 else rows - 1
        for layer in range(depth):
            across_it = loc_x[face, layer]
            across_it = jnp.sum(across_it * across_it, axis=0, keepdims=True)
            sum_x[face, layer : layer + 1] = sums[layer][edge : edge + 1] - across_it
        copy(SUMS, face).start()
    for face in range(2, 4):
        edge = 0 if face == 2 else cols - 1
        sum_y[face - 2] = per_pair(columns_of(sums, edge))
        copy(SUMS, face).start()

    for face in range(2, 4):
        wait_for(LOCAL, face)
        next_y[face - 2] = got_loc_y[face - 2] + LINK * rim_y[face - 2]
        scatter(face, None, LINK * next_y[face - 2], halo2)

    for face in range(2):
        wait_for(RIM, face)
        scatter(face, lambda layer, k: got_rim_x[face, layer, k : k + 1], None)
    update(totals(False))

    for face in range(2):
        wait_for(LOCAL, face)
        for layer in range(depth):
            next_x[face, layer] = got_loc_x[face, layer] + LINK * rim_x[face, layer]
        scatter(face, lambda layer, k: next_x[face, layer, k : k + 1], None, halo2)
    update(totals(False, halo2))

    for face in range(2):
        wait_for(CORNER, face)
    for face in range(FACES):
        wait_for(BEHIND, face)
        wait_for(SUMS, face)
        if face < 2:
            rims = [next_x[face, layer] for layer in range(depth)]
            for layer in range(depth):
                r = rims[layer]
                beside = got_row_x[face, layer] + loc_x[face, layer] + LINK * got_rim_x[face, layer]
                total = got_sum_x[face, layer : layer + 1] + jnp.sum(r * r, axis=0, keepdims=True)
                next_x[face, layer] = step_x(r, layer, rims, jnp.broadcast_to(total, r.shape), beside)
            scatter(face, lambda layer, k: next_x[face, layer, k : k + 1], None)
        else:
            beside = got_row_y[face - 2, 0] + loc_y[face - 2] + LINK * got_rim_y[face - 2]
            total = got_sum_y[face - 2]
            for other in range(2):
                h, g = got_cor_x[other, face - 2], got_row_y[face - 2, 1 + other, 0:SHARED]
                more = jnp.sum(LINK * h * (2.0 * g + LINK * h), axis=0, keepdims=True)
                more = per_pair(jnp.broadcast_to(more, (rows, cols)))
                total = total + jnp.where(row == (0 if other == 0 else rows - 1), more, 0.0)
            scatter(face, None, LINK * step_y(next_y[face - 2], total, beside))

    def finish(slot, carry):
        held_pair = tab[0, slot]
        for layer in range(depth):
            at = tile(slot, layer)
            out[at] = local[at] + halo[tile(held_pair, layer)]
        return carry

    lax.fori_loop(0, slots, finish, 0)
    for kind in (RIM, LOCAL, BEHIND, SUMS, CORNER):
        for face in range(FACES):
            copy(kind, face).wait_send()


def solution(mesh):
    nx, ny = mesh.shape["gx"], mesh.shape["gy"]

    def on_device(order_params, grain_ids, channel_maps, zplanes):
        slots, depth, rows, cols = order_params.shape
        tiles = (slots * depth, rows, cols)
        rim_x = pltpu.VMEM((2, depth, SHARED, cols), jnp.float32)
        sum_x = pltpu.VMEM((2, depth, cols), jnp.float32)
        rim_y = pltpu.VMEM((2, rows, cols), jnp.float32)
        row_y = pltpu.VMEM((2, 3, rows, cols), jnp.float32)
        ice_x = pltpu.VMEM((2, 2, SHARED, cols), jnp.float32)
        corner = pltpu.VMEM((2, 2, SHARED, cols), jnp.float32)
        operands = (channel_maps.reshape(FACES, slots), grain_ids.reshape(slots), zplanes, order_params.reshape(tiles))
        result = pl.pallas_call(
            functools.partial(kernel, slots, depth, nx, ny),
            out_shape=jax.ShapeDtypeStruct(tiles, jnp.float32),
            in_specs=[pl.BlockSpec(memory_space=pltpu.HBM)] * 4,
            out_specs=pl.BlockSpec(memory_space=pltpu.VMEM),
            scratch_shapes=[
                pltpu.VMEM(((slots + 1) * depth, rows, cols), jnp.float32),
                pltpu.VMEM(((slots + 1) * depth, rows, cols), jnp.float32),
                pltpu.VMEM(((FACES * SHARED + 1) * depth, rows, cols), jnp.float32),
                pltpu.VMEM(((FACES * SHARED + 1) * depth, rows, cols), jnp.float32),
                pltpu.VMEM((FACES, slots), jnp.int32),
                pltpu.VMEM((rows, cols), jnp.int32),
                pltpu.VMEM((rows, cols), jnp.int32),
                pltpu.SMEM((rows, cols), jnp.int32),
                pltpu.SMEM((slots,), jnp.int32),
                pltpu.VMEM((2, rows, cols), jnp.int32),
                rim_x, rim_x, rim_x, rim_x, rim_x, rim_x, sum_x, sum_x,
                rim_y, rim_y, rim_y, rim_y, row_y, row_y, rim_y, rim_y,
                rim_x, rim_y, ice_x, corner, corner, corner,
                pltpu.SemaphoreType.DMA((5,)),
                pltpu.SemaphoreType.DMA((5, FACES)),
                pltpu.SemaphoreType.DMA((5, FACES)),
            ],
            compiler_params=pltpu.CompilerParams(
                collective_id=0, has_side_effects=True, vmem_limit_bytes=16 * 2**20
            ),
        )(*[pltpu.with_memory_space_constraint(x, pltpu.HBM) for x in operands])
        return result.reshape(order_params.shape)

    in_specs = (
        P(None, None, "gx", "gy"),
        P("gx", "gy", None),
        P("gx", "gy", None, None),
        P(None, "gx", "gy"),
    )
    return jax.shard_map(
        on_device, mesh=mesh, in_specs=in_specs, out_specs=P(None, None, "gx", "gy"), check_vma=False
    )
```

```python
import functools

import jax
import jax.numpy as jnp
from jax import lax
from jax.experimental import pallas as pl
from jax.experimental.pallas import tpu as pltpu
from jax.sharding import PartitionSpec as P

SHARED = 6
FACES = 4
MESH = pl.DeviceIdType.MESH

SELF = 0.45
TOTAL = 0.15
LINK = 0.1

RIM, LOCAL, BEHIND, SUMS, CORNER = 0, 1, 2, 3, 4
UNROLL = 8


def kernel(slots, depth, nx, ny, maps_in, grains_in, planes_in, start, out, field, local, halo, halo2, maps, key_box, table, tab,
           grains, planes, rim_x, got_rim_x, loc_x, got_loc_x, row_x, got_row_x, sum_x, got_sum_x, rim_y, got_rim_y, loc_y,
           got_loc_y, row_y, got_row_y, sum_y, got_sum_y, next_x, next_y, ice_x, cor_y, got_cor_y, got_cor_x, load_sem, send_sem, recv_sem):
    rows, cols = 8, 128
    i, j = lax.axis_index("gx"), lax.axis_index("gy")
    across = (
        (lax.rem(i + nx - 1, nx), j),
        (lax.rem(i + 1, nx), j),
        (i, lax.rem(j + ny - 1, ny)),
        (i, lax.rem(j + 1, ny)),
    )
    barrier = pltpu.get_barrier_semaphore()
    for device in across:
        pl.semaphore_signal(barrier, inc=1, device_id=device, device_id_type=MESH)
    loads = [
        pltpu.make_async_copy(maps_in, maps, load_sem.at[0]),
        pltpu.make_async_copy(start, field.at[pl.ds(0, slots * depth)], load_sem.at[1]),
        pltpu.make_async_copy(grains_in, grains, load_sem.at[2]),
        pltpu.make_async_copy(planes_in, planes, load_sem.at[3]),
    ]
    for load in loads:
        load.start()

    row = lax.broadcasted_iota(jnp.int32, (rows, cols), 0)
    col = lax.broadcasted_iota(jnp.int32, (rows, cols), 1)
    lane = col[:SHARED]
    group = lax.rem(col, depth)
    deep_row, deep_col = (lax.broadcasted_iota(jnp.int32, (depth, cols), d) for d in range(2))
    zero = jnp.zeros((rows, cols), jnp.float32)

    def tile(slot, layer):
        return slot * depth + layer

    def clear(slot, carry):
        for layer in range(depth):
            halo[tile(slot, layer)] = zero
            halo2[tile(slot, layer)] = zero
        return carry

    lax.fori_loop(0, slots + 1, clear, 0)
    for layer in range(depth):
        field[tile(slots, layer)] = zero
        local[tile(slots, layer)] = zero

    loads[0].wait()
    key_box[...] = jnp.full((rows, cols), -1, jnp.int32)
    key_box[0:FACES, 0:slots] = maps[...]
    entries = key_box[...]
    linked = entries >= 0
    upper = (row == 1) | (row == 3)
    key = jnp.where(linked, jnp.where(upper, col, entries), slots)
    rank = jnp.zeros((rows, cols), jnp.int32)
    for slot in range(slots):
        rank = rank + jnp.where(key[:, slot : slot + 1] < key, 1, 0)
    pair = jnp.where(linked & (rank < SHARED), row * SHARED + rank, FACES * SHARED)
    held = jnp.broadcast_to(jnp.min(pair, axis=0, keepdims=True), (rows, cols))
    source = jnp.full((rows, cols), slots, jnp.int32)
    for slot in range(slots):
        source = jnp.minimum(source, jnp.where(held[:, slot : slot + 1] == col, slot, slots))
    table[...] = jnp.where(row == 0, held, source)
    fetch = pltpu.make_async_copy(table, tab, load_sem.at[4])
    fetch.start()

    buffers = {
        RIM: ((rim_x, got_rim_x), (rim_y, got_rim_y)),
        LOCAL: ((loc_x, got_loc_x), (loc_y, got_loc_y)),
        BEHIND: ((row_x, got_row_x), (row_y, got_row_y)),
        SUMS: ((sum_x, got_sum_x), (sum_y, got_sum_y)),
        CORNER: (None, (cor_y, got_cor_y)),
    }

    def copy(kind, face):
        if kind == CORNER and face < 2:
            source, target = got_cor_y.at[:, face], got_cor_x.at[1 - face]
        else:
            sent, got = buffers[kind][face // 2]
            source, target = sent.at[face % 2], got.at[1 - face % 2]
        return pltpu.make_async_remote_copy(
            src_ref=source,
            dst_ref=target,
            send_sem=send_sem.at[kind, face],
            recv_sem=recv_sem.at[kind, face ^ 1],
            device_id=across[face],
            device_id_type=MESH,
        )

    def wait_for(kind, face):
        copy(kind, face ^ 1).wait_recv()

    def pair_slot(face, k):
        return tab[1, face * SHARED + k]

    def grain_of(slot):
        grain = grains[jnp.minimum(slot, slots - 1)]
        return jnp.where((grain >= 0) & (slot < slots), grain, -1)

    def gather_columns(face, column, tiles):
        packed = zero
        for k in range(SHARED):
            slot = pair_slot(face, k)
            for layer in range(depth):
                place = k * depth + layer
                moved = pltpu.roll(tiles[tile(slot, layer)], (place - column) % cols, 1)
                packed = jnp.where(col == place, moved, packed)
        return packed

    def corners(rims, column):
        packed = jnp.zeros((SHARED, cols), jnp.float32)
        for layer in range(depth):
            packed = jnp.where(lane == layer, pltpu.roll(rims[layer], (layer - column) % cols, 1), packed)
        return packed

    def per_pair(layers):
        two = layers + pltpu.roll(layers, depth, 1)
        four = two + pltpu.roll(two, 2 * depth, 1)
        return four + pltpu.roll(two, 4 * depth, 1)

    def columns_of(layers, column):
        packed = zero
        for layer in range(depth):
            packed = jnp.where(col == layer, pltpu.roll(layers[layer], (layer - column) % cols, 1), packed)
        return packed

    def step_x(r, layer, rims, total, beside):
        near = (
            beside
            + jnp.where(lane == cols - 1, 0.0, pltpu.roll(r, cols - 1, 1))
            + jnp.where(lane == 0, 0.0, pltpu.roll(r, 1, 1))
        )
        if layer:
            near = near + rims[layer - 1]
        if layer < depth - 1:
            near = near + rims[layer + 1]
        return r * (SELF - TOTAL * total + LINK * r * r) + LINK * near

    def step_y(r, total, beside):
        near = (
            beside
            + jnp.where(row == rows - 1, 0.0, pltpu.roll(r, rows - 1, 0))
            + jnp.where(row == 0, 0.0, pltpu.roll(r, 1, 0))
            + jnp.where(group == depth - 1, 0.0, pltpu.roll(r, cols - 1, 1))
            + jnp.where(group == 0, 0.0, pltpu.roll(r, 1, 1))
        )
        return r * (SELF - TOTAL * total + LINK * r * r) + LINK * near

    def over_pairs(packed):
        half = packed + pltpu.roll(packed, cols - 3 * depth, 1)
        whole = half + pltpu.roll(half, cols - depth, 1) + pltpu.roll(half, cols - 2 * depth, 1)
        return jnp.where(col < depth, whole, 0.0)

    def scatter(face, layer_row, packed, halo=halo):
        edge = 0 if face % 2 == 0 else (rows if face < 2 else cols) - 1
        for k in range(SHARED):
            for layer in range(depth):
                at = tile(face * SHARED + k, layer)
                if face < 2:
                    halo[at, edge : edge + 1] = LINK * layer_row(layer, k)
                else:
                    moved = pltpu.roll(packed, (edge - (k * depth + layer)) % cols, 1)
                    halo[at] = jnp.where(col == edge, moved, 0.0)

    def totals_of(tiles):
        def body(slot, sums):
            out_sums = []
            for layer in range(depth):
                value = tiles[tile(slot, layer)]
                out_sums.append(sums[layer] + value * value)
            return tuple(out_sums)

        return lax.fori_loop(0, slots, body, (zero,) * depth, unroll=UNROLL)

    def totals(halo):
        def body(slot, sums):
            held_pair = tab[0, slot]
            out_sums = []
            for layer in range(depth):
                at = tile(slot, layer)
                value = local[at] + halo[tile(held_pair, layer)]
                field[at] = value
                out_sums.append(sums[layer] + value * value)
            return tuple(out_sums)

        return lax.fori_loop(0, slots, body, (zero,) * depth, unroll=UNROLL)

    def update(sums):
        coefs = tuple(SELF - TOTAL * s for s in sums)
        below, above = planes[0], planes[1]

        def body(slot, carry):
            grain = grain_of(slot)
            values = [field[tile(slot, layer)] for layer in range(depth)]
            small = [LINK * v for v in values]
            low = jnp.where(below == grain, LINK, 0.0)
            high = jnp.where(above == grain, LINK, 0.0)
            for layer in range(depth):
                v, w = values[layer], small[layer]
                near = (
                    jnp.where(row == rows - 1, 0.0, pltpu.roll(w, rows - 1, 0))
                    + jnp.where(row == 0, 0.0, pltpu.roll(w, 1, 0))
                    + jnp.where(col == cols - 1, 0.0, pltpu.roll(w, cols - 1, 1))
                    + jnp.where(col == 0, 0.0, pltpu.roll(w, 1, 1))
                    + (small[layer - 1] if layer else low)
                    + (small[layer + 1] if layer < depth - 1 else high)
                )
                local[tile(slot, layer)] = v * (coefs[layer] + v * w) + near
            return carry

        lax.fori_loop(0, slots, body, 0, unroll=slots)

    loads[1].wait()
    sums = totals_of(field)
    fetch.wait()
    for face in range(2):
        edge = 0 if face == 0 else rows - 1
        for k in range(SHARED):
            slot = pair_slot(face, k)
            for layer in range(depth):
                rim_x[face, layer, k : k + 1] = field[tile(slot, layer), edge : edge + 1]
    for face in range(2, 4):
        rim_y[face - 2] = gather_columns(face, 0 if face == 2 else cols - 1, field)
    pl.semaphore_wait(barrier, FACES)
    for face in range(FACES):
        copy(RIM, face).start()
    for face in range(2, 4):
        for other in range(2):
            rims = [rim_x[other, layer] for layer in range(depth)]
            cor_y[face - 2, other] = corners(rims, 0 if face == 2 else cols - 1)
        copy(CORNER, face).start()

    loads[2].wait()
    loads[3].wait()
    for face in range(2):
        edge, second = (0, 1) if face == 0 else (rows - 1, rows - 2)
        for k in range(SHARED):
            slot = pair_slot(face, k)
            grain = grain_of(slot)
            for plane in range(2):
                ice_x[face, plane, k : k + 1] = jnp.where(planes[plane, edge : edge + 1] == grain, 1.0, 0.0)
            for layer in range(depth):
                row_x[face, layer, k : k + 1] = field[tile(slot, layer), second : second + 1]
        rims = [rim_x[face, layer] for layer in range(depth)]
        for layer in range(depth):
            beside = row_x[face, layer]
            if layer == 0:
                beside = beside + ice_x[face, 0]
            if layer == depth - 1:
                beside = beside + ice_x[face, 1]
            total = jnp.broadcast_to(sums[layer][edge : edge + 1], beside.shape)
            loc_x[face, layer] = step_x(rims[layer], layer, rims, total, beside)
        copy(LOCAL, face).start()
    ice_y = []
    for face in range(2, 4):
        edge, second = (0, 1) if face == 2 else (cols - 1, cols - 2)
        ice = zero
        for k in range(SHARED):
            grain = grain_of(pair_slot(face, k))
            for plane, layer in ((0, 0), (1, depth - 1)):
                place = k * depth + layer
                frozen = jnp.where(planes[plane] == grain, 1.0, 0.0)
                ice = jnp.where(col == place, pltpu.roll(frozen, (place - edge) % cols, 1), ice)
        ice_y.append(ice)
        total = per_pair(columns_of(sums, edge))
        loc_y[face - 2] = step_y(rim_y[face - 2], total, gather_columns(face, second, field) + ice)
        copy(LOCAL, face).start()

    update(sums)

    for face in range(2):
        second = 1 if face == 0 else rows - 2
        for k in range(SHARED):
            slot = pair_slot(face, k)
            for layer in range(depth):
                behind = local[tile(slot, layer), second : second + 1]
                if layer == 0:
                    behind = behind + ice_x[face, 0, k : k + 1]
                if layer == depth - 1:
                    behind = behind + ice_x[face, 1, k : k + 1]
                row_x[face, layer, k : k + 1] = behind
        copy(BEHIND, face).start()
    for face in range(2, 4):
        edge, second = (0, 1) if face == 2 else (cols - 1, cols - 2)
        row_y[face - 2, 0] = gather_columns(face, second, local) + ice_y[face - 2]
        for other in range(2):
            rims = [loc_x[other, layer] for layer in range(depth)]
            row_y[face - 2, 1 + other, 0:SHARED] = corners(rims, edge)
        copy(BEHIND, face).start()

    sums = totals_of(local)
    for face in range(2, 4):
        edge = 0 if face == 2 else cols - 1
        rims = loc_y[face - 2]
        sum_y[face - 2] = per_pair(columns_of(sums, edge) - over_pairs(rims * rims))
        copy(SUMS, face).start()
    for face in range(2):
        edge = 0 if face == 0 else rows - 1
        for layer in range(depth):
            across_it = loc_x[face, layer]
            across_it = jnp.sum(across_it * across_it, axis=0, keepdims=True)
            sum_x[face, layer : layer + 1] = sums[layer][edge : edge + 1] - across_it
    for face in range(2, 4):
        wait_for(RIM, face)
        edge = 0 if face == 2 else cols - 1
        h = got_rim_y[face - 2]
        more = over_pairs(LINK * h * (2.0 * loc_y[face - 2] + LINK * h))
        for other in range(2):
            line = more[0:1] if other == 0 else more[rows - 1 : rows]
            line = jnp.where(deep_col == deep_row, jnp.broadcast_to(line, (depth, cols)), 0.0)
            line = jnp.sum(line, axis=1, keepdims=True)
            sum_x[other] = sum_x[other] + jnp.where(deep_col == edge, jnp.broadcast_to(line, (depth, cols)), 0.0)
    for face in range(2):
        copy(SUMS, face).start()
    for face in range(2, 4):
        wait_for(CORNER, face)
    for face in range(2):
        copy(CORNER, face).start()

    for face in range(2, 4):
        scatter(face, None, LINK * got_rim_y[face - 2])

    for face in range(2, 4):
        wait_for(LOCAL, face)
        next_y[face - 2] = got_loc_y[face - 2] + LINK * rim_y[face - 2]
        scatter(face, None, LINK * next_y[face - 2], halo2)

    for face in range(2):
        wait_for(RIM, face)
        scatter(face, lambda layer, k: got_rim_x[face, layer, k : k + 1], None)
    update(totals(halo))

    for face in range(2):
        wait_for(LOCAL, face)
        for layer in range(depth):
            next_x[face, layer] = got_loc_x[face, layer] + LINK * rim_x[face, layer]
        scatter(face, lambda layer, k: next_x[face, layer, k : k + 1], None, halo2)
    update(totals(halo2))

    for face in range(2):
        wait_for(CORNER, face)
    for face in range(FACES):
        wait_for(BEHIND, face)
        wait_for(SUMS, face)
        if face < 2:
            rims = [next_x[face, layer] for layer in range(depth)]
            for layer in range(depth):
                r = rims[layer]
                beside = got_row_x[face, layer] + loc_x[face, layer] + LINK * got_rim_x[face, layer]
                total = got_sum_x[face, layer : layer + 1] + jnp.sum(r * r, axis=0, keepdims=True)
                next_x[face, layer] = step_x(r, layer, rims, jnp.broadcast_to(total, r.shape), beside)
            scatter(face, lambda layer, k: next_x[face, layer, k : k + 1], None)
        else:
            beside = got_row_y[face - 2, 0] + loc_y[face - 2] + LINK * got_rim_y[face - 2]
            rims = next_y[face - 2]
            total = got_sum_y[face - 2] + per_pair(over_pairs(rims * rims))
            for other in range(2):
                h, g = got_cor_x[other, face - 2], got_row_y[face - 2, 1 + other, 0:SHARED]
                more = jnp.sum(LINK * h * (2.0 * g + LINK * h), axis=0, keepdims=True)
                more = per_pair(jnp.broadcast_to(more, (rows, cols)))
                total = total + jnp.where(row == (0 if other == 0 else rows - 1), more, 0.0)
            scatter(face, None, LINK * step_y(next_y[face - 2], total, beside))

    def finish(slot, carry):
        held_pair = tab[0, slot]
        for layer in range(depth):
            at = tile(slot, layer)
            out[at] = local[at] + halo[tile(held_pair, layer)]
        return carry

    lax.fori_loop(0, slots, finish, 0)
    for kind in (RIM, LOCAL, BEHIND, SUMS, CORNER):
        for face in range(FACES):
            copy(kind, face).wait_send()


def solution(mesh):
    nx, ny = mesh.shape["gx"], mesh.shape["gy"]

    def on_device(order_params, grain_ids, channel_maps, zplanes):
        slots, depth, rows, cols = order_params.shape
        tiles = (slots * depth, rows, cols)
        rim_x = pltpu.VMEM((2, depth, SHARED, cols), jnp.float32)
        sum_x = pltpu.VMEM((2, depth, cols), jnp.float32)
        rim_y = pltpu.VMEM((2, rows, cols), jnp.float32)
        row_y = pltpu.VMEM((2, 3, rows, cols), jnp.float32)
        ice_x = pltpu.VMEM((2, 2, SHARED, cols), jnp.float32)
        corner = pltpu.VMEM((2, 2, SHARED, cols), jnp.float32)
        operands = (channel_maps.reshape(FACES, slots), grain_ids.reshape(slots), zplanes, order_params.reshape(tiles))
        result = pl.pallas_call(
            functools.partial(kernel, slots, depth, nx, ny),
            out_shape=jax.ShapeDtypeStruct(tiles, jnp.float32),
            in_specs=[pl.BlockSpec(memory_space=pltpu.HBM)] * 4,
            out_specs=pl.BlockSpec(memory_space=pltpu.VMEM),
            scratch_shapes=[
                pltpu.VMEM(((slots + 1) * depth, rows, cols), jnp.float32),
                pltpu.VMEM(((slots + 1) * depth, rows, cols), jnp.float32),
                pltpu.VMEM(((FACES * SHARED + 1) * depth, rows, cols), jnp.float32),
                pltpu.VMEM(((FACES * SHARED + 1) * depth, rows, cols), jnp.float32),
                pltpu.VMEM((FACES, slots), jnp.int32),
                pltpu.VMEM((rows, cols), jnp.int32),
                pltpu.VMEM((rows, cols), jnp.int32),
                pltpu.SMEM((rows, cols), jnp.int32),
                pltpu.SMEM((slots,), jnp.int32),
                pltpu.VMEM((2, rows, cols), jnp.int32),
                rim_x, rim_x, rim_x, rim_x, rim_x, rim_x, sum_x, sum_x,
                rim_y, rim_y, rim_y, rim_y, row_y, row_y, rim_y, rim_y,
                rim_x, rim_y, ice_x, corner, corner, corner,
                pltpu.SemaphoreType.DMA((5,)),
                pltpu.SemaphoreType.DMA((5, FACES)),
                pltpu.SemaphoreType.DMA((5, FACES)),
            ],
            compiler_params=pltpu.CompilerParams(
                collective_id=0, has_side_effects=True, vmem_limit_bytes=16 * 2**20
            ),
        )(*[pltpu.with_memory_space_constraint(x, pltpu.HBM) for x in operands])
        return result.reshape(order_params.shape)

    in_specs = (
        P(None, None, "gx", "gy"),
        P("gx", "gy", None),
        P("gx", "gy", None, None),
        P(None, "gx", "gy"),
    )
    return jax.shard_map(
        on_device, mesh=mesh, in_specs=in_specs, out_specs=P(None, None, "gx", "gy"), check_vma=False
    )
```

```python
import functools

import jax
import jax.numpy as jnp
from jax import lax
from jax.experimental import pallas as pl
from jax.experimental.pallas import tpu as pltpu
from jax.sharding import PartitionSpec as P

SHARED = 6
FACES = 4
MESH = pl.DeviceIdType.MESH

SELF = 0.45
TOTAL = 0.15
LINK = 0.1

RIM, LOCAL, BEHIND, SUMS, CORNER = 0, 1, 2, 3, 4
UNROLL = 8


def kernel(slots, depth, nx, ny, maps_in, grains_in, planes_in, start, out, field, local, halo, halo2, maps, key_box, table, tab,
           grains, planes, rim_x, got_rim_x, loc_x, got_loc_x, row_x, got_row_x, sum_x, got_sum_x, rim_y, got_rim_y, loc_y,
           got_loc_y, row_y, got_row_y, sum_y, got_sum_y, next_x, next_y, ice_x, cor_y, got_cor_y, got_cor_x, load_sem, send_sem, recv_sem):
    rows, cols = 8, 128
    i, j = lax.axis_index("gx"), lax.axis_index("gy")
    across = (
        (lax.rem(i + nx - 1, nx), j),
        (lax.rem(i + 1, nx), j),
        (i, lax.rem(j + ny - 1, ny)),
        (i, lax.rem(j + 1, ny)),
    )
    barrier = pltpu.get_barrier_semaphore()
    for device in across:
        pl.semaphore_signal(barrier, inc=1, device_id=device, device_id_type=MESH)
    loads = [
        pltpu.make_async_copy(maps_in, maps, load_sem.at[0]),
        pltpu.make_async_copy(start, field.at[pl.ds(0, slots * depth)], load_sem.at[1]),
        pltpu.make_async_copy(grains_in, grains, load_sem.at[2]),
        pltpu.make_async_copy(planes_in, planes, load_sem.at[3]),
    ]
    for load in loads:
        load.start()

    row = lax.broadcasted_iota(jnp.int32, (rows, cols), 0)
    col = lax.broadcasted_iota(jnp.int32, (rows, cols), 1)
    lane = col[:SHARED]
    group = lax.rem(col, depth)
    deep_row, deep_col = (lax.broadcasted_iota(jnp.int32, (depth, cols), d) for d in range(2))
    zero = jnp.zeros((rows, cols), jnp.float32)

    def tile(slot, layer):
        return slot * depth + layer

    def clear(slot, carry):
        for layer in range(depth):
            halo[tile(slot, layer)] = zero
            halo2[tile(slot, layer)] = zero
        return carry

    lax.fori_loop(0, slots + 1, clear, 0)
    for layer in range(depth):
        field[tile(slots, layer)] = zero
        local[tile(slots, layer)] = zero

    loads[0].wait()
    key_box[...] = jnp.full((rows, cols), -1, jnp.int32)
    key_box[0:FACES, 0:slots] = maps[...]
    entries = key_box[...]
    linked = entries >= 0
    upper = (row == 1) | (row == 3)
    key = jnp.where(linked, jnp.where(upper, col, entries), slots)
    rank = jnp.zeros((rows, cols), jnp.int32)
    for slot in range(slots):
        rank = rank + jnp.where(key[:, slot : slot + 1] < key, 1, 0)
    pair = jnp.where(linked & (rank < SHARED), row * SHARED + rank, FACES * SHARED)
    held = jnp.broadcast_to(jnp.min(pair, axis=0, keepdims=True), (rows, cols))
    source = jnp.full((rows, cols), slots, jnp.int32)
    for slot in range(slots):
        source = jnp.minimum(source, jnp.where(held[:, slot : slot + 1] == col, slot, slots))
    table[...] = jnp.where(row == 0, held, source)
    fetch = pltpu.make_async_copy(table, tab, load_sem.at[4])
    fetch.start()

    buffers = {
        RIM: ((rim_x, got_rim_x), (rim_y, got_rim_y)),
        LOCAL: ((loc_x, got_loc_x), (loc_y, got_loc_y)),
        BEHIND: ((row_x, got_row_x), (row_y, got_row_y)),
        SUMS: ((sum_x, got_sum_x), (sum_y, got_sum_y)),
        CORNER: (None, (cor_y, got_cor_y)),
    }

    def copy(kind, face):
        if kind == CORNER and face < 2:
            source, target = got_cor_y.at[:, face], got_cor_x.at[1 - face]
        else:
            sent, got = buffers[kind][face // 2]
            source, target = sent.at[face % 2], got.at[1 - face % 2]
        return pltpu.make_async_remote_copy(
            src_ref=source,
            dst_ref=target,
            send_sem=send_sem.at[kind, face],
            recv_sem=recv_sem.at[kind, face ^ 1],
            device_id=across[face],
            device_id_type=MESH,
        )

    def wait_for(kind, face):
        copy(kind, face ^ 1).wait_recv()

    def pair_slot(face, k):
        return tab[1, face * SHARED + k]

    def grain_of(slot):
        grain = grains[jnp.minimum(slot, slots - 1)]
        return jnp.where((grain >= 0) & (slot < slots), grain, -1)

    def gather_columns(face, column, tiles):
        packed = zero
        for k in range(SHARED):
            slot = pair_slot(face, k)
            for layer in range(depth):
                place = k * depth + layer
                moved = pltpu.roll(tiles[tile(slot, layer)], (place - column) % cols, 1)
                packed = jnp.where(col == place, moved, packed)
        return packed

    def corners(rims, column):
        packed = jnp.zeros((SHARED, cols), jnp.float32)
        for layer in range(depth):
            packed = jnp.where(lane == layer, pltpu.roll(rims[layer], (layer - column) % cols, 1), packed)
        return packed

    def per_pair(layers):
        two = layers + pltpu.roll(layers, depth, 1)
        four = two + pltpu.roll(two, 2 * depth, 1)
        return four + pltpu.roll(two, 4 * depth, 1)

    def columns_of(layers, column):
        packed = zero
        for layer in range(depth):
            packed = jnp.where(col == layer, pltpu.roll(layers[layer], (layer - column) % cols, 1), packed)
        return packed

    def step_x(r, layer, rims, total, beside):
        near = (
            beside
            + jnp.where(lane == cols - 1, 0.0, pltpu.roll(r, cols - 1, 1))
            + jnp.where(lane == 0, 0.0, pltpu.roll(r, 1, 1))
        )
        if layer:
            near = near + rims[layer - 1]
        if layer < depth - 1:
            near = near + rims[layer + 1]
        return r * (SELF - TOTAL * total + LINK * r * r) + LINK * near

    def step_y(r, total, beside):
        near = (
            beside
            + jnp.where(row == rows - 1, 0.0, pltpu.roll(r, rows - 1, 0))
            + jnp.where(row == 0, 0.0, pltpu.roll(r, 1, 0))
            + jnp.where(group == depth - 1, 0.0, pltpu.roll(r, cols - 1, 1))
            + jnp.where(group == 0, 0.0, pltpu.roll(r, 1, 1))
        )
        return r * (SELF - TOTAL * total + LINK * r * r) + LINK * near

    def over_pairs(packed):
        half = packed + pltpu.roll(packed, cols - 3 * depth, 1)
        whole = half + pltpu.roll(half, cols - depth, 1) + pltpu.roll(half, cols - 2 * depth, 1)
        return jnp.where(col < depth, whole, 0.0)

    def scatter(face, layer_row, packed, halo=halo):
        edge = 0 if face % 2 == 0 else (rows if face < 2 else cols) - 1
        for k in range(SHARED):
            for layer in range(depth):
                at = tile(face * SHARED + k, layer)
                if face < 2:
                    halo[at, edge : edge + 1] = LINK * layer_row(layer, k)
                else:
                    moved = pltpu.roll(packed, (edge - (k * depth + layer)) % cols, 1)
                    halo[at] = jnp.where(col == edge, moved, 0.0)

    def totals_of(tiles):
        def body(slot, sums):
            out_sums = []
            for layer in range(depth):
                value = tiles[tile(slot, layer)]
                out_sums.append(sums[layer] + value * value)
            return tuple(out_sums)

        return lax.fori_loop(0, slots, body, (zero,) * depth, unroll=UNROLL)

    def totals(halo):
        def body(slot, sums):
            held_pair = tab[0, slot]
            out_sums = []
            for layer in range(depth):
                at = tile(slot, layer)
                value = local[at] + halo[tile(held_pair, layer)]
                field[at] = value
                out_sums.append(sums[layer] + value * value)
            return tuple(out_sums)

        return lax.fori_loop(0, slots, body, (zero,) * depth, unroll=UNROLL)

    def update(sums):
        coefs = tuple(SELF - TOTAL * s for s in sums)
        below, above = planes[0], planes[1]
        part_lane, into_lane = (lax.broadcasted_iota(jnp.int32, (2 * cols, cols), d) for d in range(2))
        apart = lax.rem(part_lane, cols) - into_lane
        band = jnp.where((apart == 1) | (apart == -1), 1.0, 0.0).astype(jnp.bfloat16)

        def body(slot, carry):
            grain = grain_of(slot)
            values = [field[tile(slot, layer)] for layer in range(depth)]
            small = [LINK * v for v in values]
            low = jnp.where(below == grain, LINK, 0.0)
            high = jnp.where(above == grain, LINK, 0.0)
            stack = jnp.concatenate(small, axis=0)
            big = stack.astype(jnp.bfloat16)
            rest = (stack - big.astype(jnp.float32)).astype(jnp.bfloat16)
            side = jnp.dot(jnp.concatenate([big, rest], axis=1), band, preferred_element_type=jnp.float32)
            for layer in range(depth):
                v, w = values[layer], small[layer]
                near = (
                    jnp.where(row == rows - 1, 0.0, pltpu.roll(w, rows - 1, 0))
                    + jnp.where(row == 0, 0.0, pltpu.roll(w, 1, 0))
                    + side[rows * layer : rows * layer + rows]
                    + (small[layer - 1] if layer else low)
                    + (small[layer + 1] if layer < depth - 1 else high)
                )
                local[tile(slot, layer)] = v * (coefs[layer] + v * w) + near
            return carry

        lax.fori_loop(0, slots, body, 0, unroll=slots)

    loads[1].wait()
    sums = totals_of(field)
    fetch.wait()
    for face in range(2):
        edge = 0 if face == 0 else rows - 1
        for k in range(SHARED):
            slot = pair_slot(face, k)
            for layer in range(depth):
                rim_x[face, layer, k : k + 1] = field[tile(slot, layer), edge : edge + 1]
    for face in range(2, 4):
        rim_y[face - 2] = gather_columns(face, 0 if face == 2 else cols - 1, field)
    pl.semaphore_wait(barrier, FACES)
    for face in range(FACES):
        copy(RIM, face).start()
    for face in range(2, 4):
        for other in range(2):
            rims = [rim_x[other, layer] for layer in range(depth)]
            cor_y[face - 2, other] = corners(rims, 0 if face == 2 else cols - 1)
        copy(CORNER, face).start()

    loads[2].wait()
    loads[3].wait()
    for face in range(2):
        edge, second = (0, 1) if face == 0 else (rows - 1, rows - 2)
        for k in range(SHARED):
            slot = pair_slot(face, k)
            grain = grain_of(slot)
            for plane in range(2):
                ice_x[face, plane, k : k + 1] = jnp.where(planes[plane, edge : edge + 1] == grain, 1.0, 0.0)
            for layer in range(depth):
                row_x[face, layer, k : k + 1] = field[tile(slot, layer), second : second + 1]
        rims = [rim_x[face, layer] for layer in range(depth)]
        for layer in range(depth):
            beside = row_x[face, layer]
            if layer == 0:
                beside = beside + ice_x[face, 0]
            if layer == depth - 1:
                beside = beside + ice_x[face, 1]
            total = jnp.broadcast_to(sums[layer][edge : edge + 1], beside.shape)
            loc_x[face, layer] = step_x(rims[layer], layer, rims, total, beside)
        copy(LOCAL, face).start()
    ice_y = []
    for face in range(2, 4):
        edge, second = (0, 1) if face == 2 else (cols - 1, cols - 2)
        ice = zero
        for k in range(SHARED):
            grain = grain_of(pair_slot(face, k))
            for plane, layer in ((0, 0), (1, depth - 1)):
                place = k * depth + layer
                frozen = jnp.where(planes[plane] == grain, 1.0, 0.0)
                ice = jnp.where(col == place, pltpu.roll(frozen, (place - edge) % cols, 1), ice)
        ice_y.append(ice)
        total = per_pair(columns_of(sums, edge))
        loc_y[face - 2] = step_y(rim_y[face - 2], total, gather_columns(face, second, field) + ice)
        copy(LOCAL, face).start()

    update(sums)

    for face in range(2):
        second = 1 if face == 0 else rows - 2
        for k in range(SHARED):
            slot = pair_slot(face, k)
            for layer in range(depth):
                behind = local[tile(slot, layer), second : second + 1]
                if layer == 0:
                    behind = behind + ice_x[face, 0, k : k + 1]
                if layer == depth - 1:
                    behind = behind + ice_x[face, 1, k : k + 1]
                row_x[face, layer, k : k + 1] = behind
        copy(BEHIND, face).start()
    for face in range(2, 4):
        edge, second = (0, 1) if face == 2 else (cols - 1, cols - 2)
        row_y[face - 2, 0] = gather_columns(face, second, local) + ice_y[face - 2]
        for other in range(2):
            rims = [loc_x[other, layer] for layer in range(depth)]
            row_y[face - 2, 1 + other, 0:SHARED] = corners(rims, edge)
        copy(BEHIND, face).start()

    sums = totals_of(local)
    for face in range(2, 4):
        edge = 0 if face == 2 else cols - 1
        rims = loc_y[face - 2]
        sum_y[face - 2] = per_pair(columns_of(sums, edge) - over_pairs(rims * rims))
        copy(SUMS, face).start()
    for face in range(2):
        edge = 0 if face == 0 else rows - 1
        for layer in range(depth):
            across_it = loc_x[face, layer]
            across_it = jnp.sum(across_it * across_it, axis=0, keepdims=True)
            sum_x[face, layer : layer + 1] = sums[layer][edge : edge + 1] - across_it
    for face in range(2, 4):
        wait_for(RIM, face)
        edge = 0 if face == 2 else cols - 1
        h = got_rim_y[face - 2]
        more = over_pairs(LINK * h * (2.0 * loc_y[face - 2] + LINK * h))
        for other in range(2):
            line = more[0:1] if other == 0 else more[rows - 1 : rows]
            line = jnp.where(deep_col == deep_row, jnp.broadcast_to(line, (depth, cols)), 0.0)
            line = jnp.sum(line, axis=1, keepdims=True)
            sum_x[other] = sum_x[other] + jnp.where(deep_col == edge, jnp.broadcast_to(line, (depth, cols)), 0.0)
    for face in range(2):
        copy(SUMS, face).start()
    for face in range(2, 4):
        wait_for(CORNER, face)
    for face in range(2):
        copy(CORNER, face).start()

    for face in range(2, 4):
        scatter(face, None, LINK * got_rim_y[face - 2])

    for face in range(2, 4):
        wait_for(LOCAL, face)
        next_y[face - 2] = got_loc_y[face - 2] + LINK * rim_y[face - 2]
        scatter(face, None, LINK * next_y[face - 2], halo2)

    for face in range(2):
        wait_for(RIM, face)
        scatter(face, lambda layer, k: got_rim_x[face, layer, k : k + 1], None)
    update(totals(halo))

    for face in range(2):
        wait_for(LOCAL, face)
        for layer in range(depth):
            next_x[face, layer] = got_loc_x[face, layer] + LINK * rim_x[face, layer]
        scatter(face, lambda layer, k: next_x[face, layer, k : k + 1], None, halo2)
    update(totals(halo2))

    for face in range(2):
        wait_for(CORNER, face)
    for face in range(FACES):
        wait_for(BEHIND, face)
        wait_for(SUMS, face)
        if face < 2:
            rims = [next_x[face, layer] for layer in range(depth)]
            for layer in range(depth):
                r = rims[layer]
                beside = got_row_x[face, layer] + loc_x[face, layer] + LINK * got_rim_x[face, layer]
                total = got_sum_x[face, layer : layer + 1] + jnp.sum(r * r, axis=0, keepdims=True)
                next_x[face, layer] = step_x(r, layer, rims, jnp.broadcast_to(total, r.shape), beside)
            scatter(face, lambda layer, k: next_x[face, layer, k : k + 1], None)
        else:
            beside = got_row_y[face - 2, 0] + loc_y[face - 2] + LINK * got_rim_y[face - 2]
            rims = next_y[face - 2]
            total = got_sum_y[face - 2] + per_pair(over_pairs(rims * rims))
            for other in range(2):
                h, g = got_cor_x[other, face - 2], got_row_y[face - 2, 1 + other, 0:SHARED]
                more = jnp.sum(LINK * h * (2.0 * g + LINK * h), axis=0, keepdims=True)
                more = per_pair(jnp.broadcast_to(more, (rows, cols)))
                total = total + jnp.where(row == (0 if other == 0 else rows - 1), more, 0.0)
            scatter(face, None, LINK * step_y(next_y[face - 2], total, beside))

    def finish(slot, carry):
        held_pair = tab[0, slot]
        for layer in range(depth):
            at = tile(slot, layer)
            out[at] = local[at] + halo[tile(held_pair, layer)]
        return carry

    lax.fori_loop(0, slots, finish, 0)
    for kind in (RIM, LOCAL, BEHIND, SUMS, CORNER):
        for face in range(FACES):
            copy(kind, face).wait_send()


def solution(mesh):
    nx, ny = mesh.shape["gx"], mesh.shape["gy"]

    def on_device(order_params, grain_ids, channel_maps, zplanes):
        slots, depth, rows, cols = order_params.shape
        tiles = (slots * depth, rows, cols)
        rim_x = pltpu.VMEM((2, depth, SHARED, cols), jnp.float32)
        sum_x = pltpu.VMEM((2, depth, cols), jnp.float32)
        rim_y = pltpu.VMEM((2, rows, cols), jnp.float32)
        row_y = pltpu.VMEM((2, 3, rows, cols), jnp.float32)
        ice_x = pltpu.VMEM((2, 2, SHARED, cols), jnp.float32)
        corner = pltpu.VMEM((2, 2, SHARED, cols), jnp.float32)
        operands = (channel_maps.reshape(FACES, slots), grain_ids.reshape(slots), zplanes, order_params.reshape(tiles))
        result = pl.pallas_call(
            functools.partial(kernel, slots, depth, nx, ny),
            out_shape=jax.ShapeDtypeStruct(tiles, jnp.float32),
            in_specs=[pl.BlockSpec(memory_space=pltpu.HBM)] * 4,
            out_specs=pl.BlockSpec(memory_space=pltpu.VMEM),
            scratch_shapes=[
                pltpu.VMEM(((slots + 1) * depth, rows, cols), jnp.float32),
                pltpu.VMEM(((slots + 1) * depth, rows, cols), jnp.float32),
                pltpu.VMEM(((FACES * SHARED + 1) * depth, rows, cols), jnp.float32),
                pltpu.VMEM(((FACES * SHARED + 1) * depth, rows, cols), jnp.float32),
                pltpu.VMEM((FACES, slots), jnp.int32),
                pltpu.VMEM((rows, cols), jnp.int32),
                pltpu.VMEM((rows, cols), jnp.int32),
                pltpu.SMEM((rows, cols), jnp.int32),
                pltpu.SMEM((slots,), jnp.int32),
                pltpu.VMEM((2, rows, cols), jnp.int32),
                rim_x, rim_x, rim_x, rim_x, rim_x, rim_x, sum_x, sum_x,
                rim_y, rim_y, rim_y, rim_y, row_y, row_y, rim_y, rim_y,
                rim_x, rim_y, ice_x, corner, corner, corner,
                pltpu.SemaphoreType.DMA((5,)),
                pltpu.SemaphoreType.DMA((5, FACES)),
                pltpu.SemaphoreType.DMA((5, FACES)),
            ],
            compiler_params=pltpu.CompilerParams(
                collective_id=0, has_side_effects=True, vmem_limit_bytes=16 * 2**20
            ),
        )(*[pltpu.with_memory_space_constraint(x, pltpu.HBM) for x in operands])
        return result.reshape(order_params.shape)

    in_specs = (
        P(None, None, "gx", "gy"),
        P("gx", "gy", None),
        P("gx", "gy", None, None),
        P(None, "gx", "gy"),
    )
    return jax.shard_map(
        on_device, mesh=mesh, in_specs=in_specs, out_specs=P(None, None, "gx", "gy"), check_vma=False
    )
```

```python
import functools

import jax
import jax.numpy as jnp
from jax import lax
from jax.experimental import pallas as pl
from jax.experimental.pallas import tpu as pltpu
from jax.sharding import PartitionSpec as P

SHARED = 6
FACES = 4
MESH = pl.DeviceIdType.MESH

SELF = 0.45
TOTAL = 0.15
LINK = 0.1

RIM, LOCAL, BEHIND, SUMS, CORNER = 0, 1, 2, 3, 4
UNROLL = 8


def kernel(slots, depth, nx, ny, maps_in, grains_in, planes_in, start, out, field, local, halo, halo2, maps, key_box, table, tab,
           grains, planes, rim_x, got_rim_x, loc_x, got_loc_x, row_x, got_row_x, sum_x, got_sum_x, rim_y, got_rim_y, loc_y,
           got_loc_y, row_y, got_row_y, sum_y, got_sum_y, next_x, next_y, ice_x, cor_y, got_cor_y, got_cor_x, load_sem, send_sem, recv_sem):
    rows, cols = 8, 128
    i, j = lax.axis_index("gx"), lax.axis_index("gy")
    across = (
        (lax.rem(i + nx - 1, nx), j),
        (lax.rem(i + 1, nx), j),
        (i, lax.rem(j + ny - 1, ny)),
        (i, lax.rem(j + 1, ny)),
    )
    barrier = pltpu.get_barrier_semaphore()
    for device in across:
        pl.semaphore_signal(barrier, inc=1, device_id=device, device_id_type=MESH)
    loads = [
        pltpu.make_async_copy(maps_in, maps, load_sem.at[0]),
        pltpu.make_async_copy(start, field.at[pl.ds(0, slots * depth)], load_sem.at[1]),
        pltpu.make_async_copy(grains_in, grains, load_sem.at[2]),
        pltpu.make_async_copy(planes_in, planes, load_sem.at[3]),
    ]
    for load in loads:
        load.start()

    row = lax.broadcasted_iota(jnp.int32, (rows, cols), 0)
    col = lax.broadcasted_iota(jnp.int32, (rows, cols), 1)
    lane = col[:SHARED]
    group = lax.rem(col, depth)
    deep_row, deep_col = (lax.broadcasted_iota(jnp.int32, (depth, cols), d) for d in range(2))
    zero = jnp.zeros((rows, cols), jnp.float32)

    def tile(slot, layer):
        return slot * depth + layer

    def clear(slot, carry):
        for layer in range(depth):
            halo[tile(slot, layer)] = zero
            halo2[tile(slot, layer)] = zero
        return carry

    lax.fori_loop(0, slots + 1, clear, 0)
    for layer in range(depth):
        field[tile(slots, layer)] = zero
        local[tile(slots, layer)] = zero

    loads[0].wait()
    key_box[...] = jnp.full((rows, cols), -1, jnp.int32)
    key_box[0:FACES, 0:slots] = maps[...]
    entries = key_box[...]
    linked = entries >= 0
    upper = (row == 1) | (row == 3)
    key = jnp.where(linked, jnp.where(upper, col, entries), slots)
    rank = jnp.zeros((rows, cols), jnp.int32)
    for slot in range(slots):
        rank = rank + jnp.where(key[:, slot : slot + 1] < key, 1, 0)
    pair = jnp.where(linked & (rank < SHARED), row * SHARED + rank, FACES * SHARED)
    held = jnp.broadcast_to(jnp.min(pair, axis=0, keepdims=True), (rows, cols))
    source = jnp.full((rows, cols), slots, jnp.int32)
    for slot in range(slots):
        source = jnp.minimum(source, jnp.where(held[:, slot : slot + 1] == col, slot, slots))
    table[...] = jnp.where(row == 0, held, source)
    fetch = pltpu.make_async_copy(table, tab, load_sem.at[4])
    fetch.start()

    buffers = {
        RIM: ((rim_x, got_rim_x), (rim_y, got_rim_y)),
        LOCAL: ((loc_x, got_loc_x), (loc_y, got_loc_y)),
        BEHIND: ((row_x, got_row_x), (row_y, got_row_y)),
        SUMS: ((sum_x, got_sum_x), (sum_y, got_sum_y)),
        CORNER: (None, (cor_y, got_cor_y)),
    }

    def copy(kind, face):
        if kind == CORNER and face < 2:
            source, target = got_cor_y.at[:, face], got_cor_x.at[1 - face]
        else:
            sent, got = buffers[kind][face // 2]
            source, target = sent.at[face % 2], got.at[1 - face % 2]
        return pltpu.make_async_remote_copy(
            src_ref=source,
            dst_ref=target,
            send_sem=send_sem.at[kind, face],
            recv_sem=recv_sem.at[kind, face ^ 1],
            device_id=across[face],
            device_id_type=MESH,
        )

    def wait_for(kind, face):
        copy(kind, face ^ 1).wait_recv()

    def pair_slot(face, k):
        return tab[1, face * SHARED + k]

    def grain_of(slot):
        grain = grains[jnp.minimum(slot, slots - 1)]
        return jnp.where((grain >= 0) & (slot < slots), grain, -1)

    def gather_columns(face, column, tiles):
        packed = zero
        for k in range(SHARED):
            slot = pair_slot(face, k)
            for layer in range(depth):
                place = k * depth + layer
                moved = pltpu.roll(tiles[tile(slot, layer)], (place - column) % cols, 1)
                packed = jnp.where(col == place, moved, packed)
        return packed

    def corners(rims, column):
        packed = jnp.zeros((SHARED, cols), jnp.float32)
        for layer in range(depth):
            packed = jnp.where(lane == layer, pltpu.roll(rims[layer], (layer - column) % cols, 1), packed)
        return packed

    def per_pair(layers):
        two = layers + pltpu.roll(layers, depth, 1)
        four = two + pltpu.roll(two, 2 * depth, 1)
        return four + pltpu.roll(two, 4 * depth, 1)

    def columns_of(layers, column):
        packed = zero
        for layer in range(depth):
            packed = jnp.where(col == layer, pltpu.roll(layers[layer], (layer - column) % cols, 1), packed)
        return packed

    def step_x(r, layer, rims, total, beside):
        near = (
            beside
            + jnp.where(lane == cols - 1, 0.0, pltpu.roll(r, cols - 1, 1))
            + jnp.where(lane == 0, 0.0, pltpu.roll(r, 1, 1))
        )
        if layer:
            near = near + rims[layer - 1]
        if layer < depth - 1:
            near = near + rims[layer + 1]
        return r * (SELF - TOTAL * total + LINK * r * r) + LINK * near

    def step_y(r, total, beside):
        near = (
            beside
            + jnp.where(row == rows - 1, 0.0, pltpu.roll(r, rows - 1, 0))
            + jnp.where(row == 0, 0.0, pltpu.roll(r, 1, 0))
            + jnp.where(group == depth - 1, 0.0, pltpu.roll(r, cols - 1, 1))
            + jnp.where(group == 0, 0.0, pltpu.roll(r, 1, 1))
        )
        return r * (SELF - TOTAL * total + LINK * r * r) + LINK * near

    def over_pairs(packed):
        half = packed + pltpu.roll(packed, cols - 3 * depth, 1)
        whole = half + pltpu.roll(half, cols - depth, 1) + pltpu.roll(half, cols - 2 * depth, 1)
        return jnp.where(col < depth, whole, 0.0)

    def scatter(face, layer_row, packed, halo=halo):
        edge = 0 if face % 2 == 0 else (rows if face < 2 else cols) - 1
        for k in range(SHARED):
            for layer in range(depth):
                at = tile(face * SHARED + k, layer)
                if face < 2:
                    halo[at, edge : edge + 1] = LINK * layer_row(layer, k)
                else:
                    moved = pltpu.roll(packed, (edge - (k * depth + layer)) % cols, 1)
                    halo[at] = jnp.where(col == edge, moved, 0.0)

    def totals_of(tiles):
        def body(slot, sums):
            out_sums = []
            for layer in range(depth):
                value = tiles[tile(slot, layer)]
                out_sums.append(sums[layer] + value * value)
            return tuple(out_sums)

        return lax.fori_loop(0, slots, body, (zero,) * depth, unroll=UNROLL)

    def totals(halo):
        def body(slot, sums):
            held_pair = tab[0, slot]
            out_sums = []
            for layer in range(depth):
                at = tile(slot, layer)
                value = local[at] + halo[tile(held_pair, layer)]
                field[at] = value
                out_sums.append(sums[layer] + value * value)
            return tuple(out_sums)

        return lax.fori_loop(0, slots, body, (zero,) * depth, unroll=UNROLL)

    def update(sums):
        coefs = tuple(SELF - TOTAL * s for s in sums)
        below, above = planes[0], planes[1]
        part_lane, into_lane = (lax.broadcasted_iota(jnp.int32, (2 * cols, cols), d) for d in range(2))
        apart = lax.rem(part_lane, cols) - into_lane
        band = jnp.where((apart == 1) | (apart == -1), 1.0, 0.0).astype(jnp.bfloat16)

        def body(slot, carry):
            grain = grain_of(slot)
            values = [field[tile(slot, layer)] for layer in range(depth)]
            small = [LINK * v for v in values]
            low = jnp.where(below == grain, LINK, 0.0)
            high = jnp.where(above == grain, LINK, 0.0)
            stack = jnp.concatenate(small, axis=0)
            big = stack.astype(jnp.bfloat16)
            rest = (stack - big.astype(jnp.float32)).astype(jnp.bfloat16)
            side = jnp.dot(jnp.concatenate([big, rest], axis=1), band, preferred_element_type=jnp.float32)
            for layer in range(depth):
                v, w = values[layer], small[layer]
                near = (
                    jnp.where(row == rows - 1, 0.0, pltpu.roll(w, rows - 1, 0))
                    + jnp.where(row == 0, 0.0, pltpu.roll(w, 1, 0))
                    + side[rows * layer : rows * layer + rows]
                    + (small[layer - 1] if layer else low)
                    + (small[layer + 1] if layer < depth - 1 else high)
                )
                local[tile(slot, layer)] = v * (coefs[layer] + v * w) + near
            return carry

        lax.fori_loop(0, slots, body, 0, unroll=slots)

    loads[1].wait()
    sums = totals_of(field)
    fetch.wait()
    for face in range(2):
        edge = 0 if face == 0 else rows - 1
        for k in range(SHARED):
            slot = pair_slot(face, k)
            for layer in range(depth):
                rim_x[face, layer, k : k + 1] = field[tile(slot, layer), edge : edge + 1]
    for face in range(2, 4):
        rim_y[face - 2] = gather_columns(face, 0 if face == 2 else cols - 1, field)
    for face in range(2, 4):
        for other in range(2):
            rims = [rim_x[other, layer] for layer in range(depth)]
            cor_y[face - 2, other] = corners(rims, 0 if face == 2 else cols - 1)
    pl.semaphore_wait(barrier, FACES)
    for kind, faces in ((RIM, (2, 3)), (CORNER, (2, 3)), (RIM, (0, 1))):
        for face in faces:
            copy(kind, face).start()

    loads[2].wait()
    loads[3].wait()
    for face in range(2):
        edge, second = (0, 1) if face == 0 else (rows - 1, rows - 2)
        for k in range(SHARED):
            slot = pair_slot(face, k)
            grain = grain_of(slot)
            for plane in range(2):
                ice_x[face, plane, k : k + 1] = jnp.where(planes[plane, edge : edge + 1] == grain, 1.0, 0.0)
            for layer in range(depth):
                row_x[face, layer, k : k + 1] = field[tile(slot, layer), second : second + 1]
        rims = [rim_x[face, layer] for layer in range(depth)]
        for layer in range(depth):
            beside = row_x[face, layer]
            if layer == 0:
                beside = beside + ice_x[face, 0]
            if layer == depth - 1:
                beside = beside + ice_x[face, 1]
            total = jnp.broadcast_to(sums[layer][edge : edge + 1], beside.shape)
            loc_x[face, layer] = step_x(rims[layer], layer, rims, total, beside)
        copy(LOCAL, face).start()
    ice_y = []
    for face in range(2, 4):
        edge, second = (0, 1) if face == 2 else (cols - 1, cols - 2)
        ice = zero
        for k in range(SHARED):
            grain = grain_of(pair_slot(face, k))
            for plane, layer in ((0, 0), (1, depth - 1)):
                place = k * depth + layer
                frozen = jnp.where(planes[plane] == grain, 1.0, 0.0)
                ice = jnp.where(col == place, pltpu.roll(frozen, (place - edge) % cols, 1), ice)
        ice_y.append(ice)
        total = per_pair(columns_of(sums, edge))
        loc_y[face - 2] = step_y(rim_y[face - 2], total, gather_columns(face, second, field) + ice)
        copy(LOCAL, face).start()

    update(sums)

    for face in range(2):
        second = 1 if face == 0 else rows - 2
        for k in range(SHARED):
            slot = pair_slot(face, k)
            for layer in range(depth):
                behind = local[tile(slot, layer), second : second + 1]
                if layer == 0:
                    behind = behind + ice_x[face, 0, k : k + 1]
                if layer == depth - 1:
                    behind = behind + ice_x[face, 1, k : k + 1]
                row_x[face, layer, k : k + 1] = behind
        copy(BEHIND, face).start()
    for face in range(2, 4):
        edge, second = (0, 1) if face == 2 else (cols - 1, cols - 2)
        row_y[face - 2, 0] = gather_columns(face, second, local) + ice_y[face - 2]
        for other in range(2):
            rims = [loc_x[other, layer] for layer in range(depth)]
            row_y[face - 2, 1 + other, 0:SHARED] = corners(rims, edge)
        copy(BEHIND, face).start()

    sums = totals_of(local)
    for face in range(2, 4):
        edge = 0 if face == 2 else cols - 1
        rims = loc_y[face - 2]
        sum_y[face - 2] = per_pair(columns_of(sums, edge) - over_pairs(rims * rims))
        copy(SUMS, face).start()
    for face in range(2):
        edge = 0 if face == 0 else rows - 1
        for layer in range(depth):
            across_it = loc_x[face, layer]
            across_it = jnp.sum(across_it * across_it, axis=0, keepdims=True)
            sum_x[face, layer : layer + 1] = sums[layer][edge : edge + 1] - across_it
    for face in range(2, 4):
        wait_for(RIM, face)
        edge = 0 if face == 2 else cols - 1
        h = got_rim_y[face - 2]
        more = over_pairs(LINK * h * (2.0 * loc_y[face - 2] + LINK * h))
        for other in range(2):
            line = more[0:1] if other == 0 else more[rows - 1 : rows]
            line = jnp.where(deep_col == deep_row, jnp.broadcast_to(line, (depth, cols)), 0.0)
            line = jnp.sum(line, axis=1, keepdims=True)
            sum_x[other] = sum_x[other] + jnp.where(deep_col == edge, jnp.broadcast_to(line, (depth, cols)), 0.0)
    for face in range(2):
        copy(SUMS, face).start()
    for face in range(2, 4):
        wait_for(CORNER, face)
    for face in range(2):
        copy(CORNER, face).start()

    for face in range(2, 4):
        scatter(face, None, LINK * got_rim_y[face - 2])

    for face in range(2, 4):
        wait_for(LOCAL, face)
        next_y[face - 2] = got_loc_y[face - 2] + LINK * rim_y[face - 2]
        scatter(face, None, LINK * next_y[face - 2], halo2)

    for face in range(2):
        wait_for(RIM, face)
        scatter(face, lambda layer, k: got_rim_x[face, layer, k : k + 1], None)
    update(totals(halo))

    for face in range(2):
        wait_for(LOCAL, face)
        for layer in range(depth):
            next_x[face, layer] = got_loc_x[face, layer] + LINK * rim_x[face, layer]
        scatter(face, lambda layer, k: next_x[face, layer, k : k + 1], None, halo2)
    update(totals(halo2))

    for face in range(2):
        wait_for(CORNER, face)
    for face in range(FACES):
        wait_for(BEHIND, face)
        wait_for(SUMS, face)
        if face < 2:
            rims = [next_x[face, layer] for layer in range(depth)]
            for layer in range(depth):
                r = rims[layer]
                beside = got_row_x[face, layer] + loc_x[face, layer] + LINK * got_rim_x[face, layer]
                total = got_sum_x[face, layer : layer + 1] + jnp.sum(r * r, axis=0, keepdims=True)
                next_x[face, layer] = step_x(r, layer, rims, jnp.broadcast_to(total, r.shape), beside)
            scatter(face, lambda layer, k: next_x[face, layer, k : k + 1], None)
        else:
            beside = got_row_y[face - 2, 0] + loc_y[face - 2] + LINK * got_rim_y[face - 2]
            rims = next_y[face - 2]
            total = got_sum_y[face - 2] + per_pair(over_pairs(rims * rims))
            for other in range(2):
                h, g = got_cor_x[other, face - 2], got_row_y[face - 2, 1 + other, 0:SHARED]
                more = jnp.sum(LINK * h * (2.0 * g + LINK * h), axis=0, keepdims=True)
                more = per_pair(jnp.broadcast_to(more, (rows, cols)))
                total = total + jnp.where(row == (0 if other == 0 else rows - 1), more, 0.0)
            scatter(face, None, LINK * step_y(next_y[face - 2], total, beside))

    def finish(slot, carry):
        held_pair = tab[0, slot]
        for layer in range(depth):
            at = tile(slot, layer)
            out[at] = local[at] + halo[tile(held_pair, layer)]
        return carry

    lax.fori_loop(0, slots, finish, 0, unroll=UNROLL)
    for kind in (RIM, LOCAL, BEHIND, SUMS, CORNER):
        for face in range(FACES):
            copy(kind, face).wait_send()


def solution(mesh):
    nx, ny = mesh.shape["gx"], mesh.shape["gy"]

    def on_device(order_params, grain_ids, channel_maps, zplanes):
        slots, depth, rows, cols = order_params.shape
        tiles = (slots * depth, rows, cols)
        rim_x = pltpu.VMEM((2, depth, SHARED, cols), jnp.float32)
        sum_x = pltpu.VMEM((2, depth, cols), jnp.float32)
        rim_y = pltpu.VMEM((2, rows, cols), jnp.float32)
        row_y = pltpu.VMEM((2, 3, rows, cols), jnp.float32)
        ice_x = pltpu.VMEM((2, 2, SHARED, cols), jnp.float32)
        corner = pltpu.VMEM((2, 2, SHARED, cols), jnp.float32)
        operands = (channel_maps.reshape(FACES, slots), grain_ids.reshape(slots), zplanes, order_params.reshape(tiles))
        result = pl.pallas_call(
            functools.partial(kernel, slots, depth, nx, ny),
            out_shape=jax.ShapeDtypeStruct(tiles, jnp.float32),
            in_specs=[pl.BlockSpec(memory_space=pltpu.HBM)] * 4,
            out_specs=pl.BlockSpec(memory_space=pltpu.VMEM),
            scratch_shapes=[
                pltpu.VMEM(((slots + 1) * depth, rows, cols), jnp.float32),
                pltpu.VMEM(((slots + 1) * depth, rows, cols), jnp.float32),
                pltpu.VMEM(((FACES * SHARED + 1) * depth, rows, cols), jnp.float32),
                pltpu.VMEM(((FACES * SHARED + 1) * depth, rows, cols), jnp.float32),
                pltpu.VMEM((FACES, slots), jnp.int32),
                pltpu.VMEM((rows, cols), jnp.int32),
                pltpu.VMEM((rows, cols), jnp.int32),
                pltpu.SMEM((rows, cols), jnp.int32),
                pltpu.SMEM((slots,), jnp.int32),
                pltpu.VMEM((2, rows, cols), jnp.int32),
                rim_x, rim_x, rim_x, rim_x, rim_x, rim_x, sum_x, sum_x,
                rim_y, rim_y, rim_y, rim_y, row_y, row_y, rim_y, rim_y,
                rim_x, rim_y, ice_x, corner, corner, corner,
                pltpu.SemaphoreType.DMA((5,)),
                pltpu.SemaphoreType.DMA((5, FACES)),
                pltpu.SemaphoreType.DMA((5, FACES)),
            ],
            compiler_params=pltpu.CompilerParams(
                collective_id=0, has_side_effects=True, vmem_limit_bytes=16 * 2**20
            ),
        )(*[pltpu.with_memory_space_constraint(x, pltpu.HBM) for x in operands])
        return result.reshape(order_params.shape)

    in_specs = (
        P(None, None, "gx", "gy"),
        P("gx", "gy", None),
        P("gx", "gy", None, None),
        P(None, "gx", "gy"),
    )
    return jax.shard_map(
        on_device, mesh=mesh, in_specs=in_specs, out_specs=P(None, None, "gx", "gy"), check_vma=False
    )
```
